32 devices in a mesh: layer: 4 (over z), feat: 2 (over y), tok: 4 (over x, core).
Axes of the slice: x: 2, y: 2, z: 4, core: 2. Of those that a mesh axis runs over, the one named last changes fastest.
Arguments:
- sublevel_entries: bfloat16 [4, 1024, 1152], P('layer', 'tok'), may hold values from -6 to 6
- readin_matrix: bfloat16 [4, 1152, 8192], P('layer', None, ('feat', 'tok')), may hold values from -0.1875 to 0.1875
- readin_offset: float32 [4, 8192], P('layer', ('feat', 'tok')), may hold values from -3 to 3
- cutoff_exceeded: int32 [4, 1024, 8192], P('layer', None, ('feat', 'tok')), may hold values 0 or 1
- writeout_matrix: bfloat16 [4, 2, 8192, 1152], P('layer', None, ('feat', 'tok')), may hold values from -0.0625 to 0.0625
- hidden_block_result: bfloat16 [2, 1024, 1152], P(None, 'tok'), may hold values from -6 to 6
- writing_depth_number: int32 [2], replicated, may hold values from 0 to 3, as said below
Outputs:
- enc_grad: bfloat16 [4, 1152, 8192], P('layer', None, ('feat', 'tok'))
- dec_grad: bfloat16 [4, 2, 8192, 1152], P('layer', None, ('feat', 'tok'))
- bias_grad: float32 [4, 8192], P('layer', ('feat', 'tok'))
The draws below stay inside these ranges and needn't reach their ends.
Inputs may be any that keep to these rules, and one draw needn't show every extreme that they name: `writing_depth_number`: one of the two entries is 3 and the other is smaller; either may come first.
All inputs are finite; a program needn't handle non-finite values. No bound on the sum of `cutoff_exceeded` on one device may be relied on, other than what follows from the above.
Results may differ from the reference program's by a relative error of at most 0.007.
Values may be sent and summed in bfloat16 or wider, within the bound.
No kernel may reach another device: no remote copies, remote signals or barrier semaphores. Data moves between devices by JAX's collectives and lax.ppermute only.
A program may use at most 128 MiB of HBM per device.

```python
import math
import jax
import jax.numpy as jnp
from jax import lax

D = 1152
LATENT_WIDTH = 8192
TARGETS = 2
READ_DEPTHS = 4
POSITION_NUMBER = 1024


def draw_writing_depth_number(key, part):
    shallow = jax.random.randint(jax.random.fold_in(key, 4093), (1,), 0, READ_DEPTHS - 1).astype(jnp.int32)
    deepest = jnp.full((1,), READ_DEPTHS - 1, jnp.int32)
    flipped = jax.random.randint(jax.random.fold_in(key, 7919), (1,), 0, 2).astype(jnp.int32)
    first = flipped * deepest + (1 - flipped) * shallow
    second = flipped * shallow + (1 - flipped) * deepest
    return jnp.concatenate([first, second]).astype(jnp.int32)


def set_ends(values, rng, least, largest):
    longest = values.shape.index(max(values.shape))
    spots = []
    for shift in (0, 1):
        where = [jax.random.randint(jax.random.fold_in(rng, axis), (), 0, length) for axis, length in enumerate(values.shape)]
        where[longest] = (where[longest] + shift) % values.shape[longest]
        spots.append(tuple(where))
    return values.at[spots[0]].set(least).at[spots[1]].set(largest)


def steps_of(key, extent, split, low, largest):
    def one(position, shards_of):
        heights = jax.random.uniform(jax.random.fold_in(jax.random.fold_in(key, 6), position), (shards_of,), jnp.float32, low / len(split), largest / len(split))
        return jnp.repeat(jnp.exp(heights), extent[position] // shards_of).reshape((-1,) + (1,) * (len(extent) - position - 1))

    level = one(*split[0])
    for cut in split[1:]:
        level = level * one(*cut)
    return level


def noise(key, dims, deviation, most, split=(), held_as=jnp.bfloat16):
    result = deviation * jax.random.normal(key, dims, jnp.float32)
    if split:
        result = result * steps_of(key, dims, split, -0.22, 0.18)
    return jnp.clip(result, -most, most).astype(held_as)


def setup_inputs(seed: int = 0) -> dict:
    key_of = jax.random.split(jax.random.key(seed), 8)
    sublevel_entries = noise(key_of[0], (READ_DEPTHS, POSITION_NUMBER, D), 1.0, 6.0, ((0, 4), (1, 4)))
    readin_matrix = noise(key_of[1], (READ_DEPTHS, D, LATENT_WIDTH), D ** -0.5, 0.1875, ((0, 4), (2, 8)))
    readin_offset = noise(key_of[2], (READ_DEPTHS, LATENT_WIDTH), 0.5, 3.0, ((0, 4), (1, 8)), jnp.float32)
    cutoff_exceeded = set_ends((jax.random.randint(key_of[3], (READ_DEPTHS, POSITION_NUMBER, LATENT_WIDTH), 0, 4) < 1).astype(jnp.int32), jax.random.fold_in(key_of[3], 1), 0, 1)
    writeout_matrix = noise(key_of[4], (READ_DEPTHS, TARGETS, LATENT_WIDTH, D), LATENT_WIDTH ** -0.5, 0.0625, ((0, 4), (2, 8)))
    hidden_block_result = noise(key_of[5], (TARGETS, POSITION_NUMBER, D), 1.0, 6.0, ((1, 4),))
    writing_depth_number = draw_writing_depth_number(jax.random.fold_in(key_of[7], 71), 0)
    return {"sublevel_entries": sublevel_entries, "readin_matrix": readin_matrix, "readin_offset": readin_offset, "cutoff_exceeded": cutoff_exceeded, "writeout_matrix": writeout_matrix, "hidden_block_result": hidden_block_result, "writing_depth_number": writing_depth_number}


def reference(sublevel_entries, readin_matrix, readin_offset, cutoff_exceeded, writeout_matrix, hidden_block_result, writing_depth_number):
    inverse = 1.0 / math.sqrt(POSITION_NUMBER)
    rebuilt = -hidden_block_result.astype(jnp.float32)
    acts_list = []
    for reading_depth in range(READ_DEPTHS):
        encoded_prejump_signal = jnp.dot(sublevel_entries[reading_depth], readin_matrix[reading_depth], preferred_element_type=jnp.float32) + readin_offset[reading_depth][None, :]
        sparse_code_entries = (encoded_prejump_signal * cutoff_exceeded[reading_depth].astype(jnp.float32)).astype(jnp.bfloat16)
        acts_list.append(sparse_code_entries)
        live_mask = (reading_depth <= writing_depth_number).astype(jnp.float32)
        for desired_reconstruction in range(TARGETS):
            rebuilt = rebuilt.at[desired_reconstruction].add(live_mask[desired_reconstruction] * jnp.dot(sparse_code_entries, writeout_matrix[reading_depth, desired_reconstruction], preferred_element_type=jnp.float32))
    scaled = (rebuilt * inverse).astype(jnp.bfloat16)
    enc_list = []
    dec_list = []
    bias_list = []
    for reading_depth in range(READ_DEPTHS):
        sparse_code_entries = acts_list[reading_depth]
        live_mask = (reading_depth <= writing_depth_number).astype(jnp.float32)
        dec_rows = []
        code_sensitivity = jnp.zeros((POSITION_NUMBER, LATENT_WIDTH), jnp.float32)
        for desired_reconstruction in range(TARGETS):
            dec_rows.append((jnp.dot(sparse_code_entries.T, scaled[desired_reconstruction], preferred_element_type=jnp.float32) * live_mask[desired_reconstruction]).astype(jnp.bfloat16))
            code_sensitivity = code_sensitivity + live_mask[desired_reconstruction] * jnp.dot(scaled[desired_reconstruction], writeout_matrix[reading_depth, desired_reconstruction].T, preferred_element_type=jnp.float32)
        prejump_sensitivity = code_sensitivity * cutoff_exceeded[reading_depth].astype(jnp.float32)
        bias_list.append(lax.optimization_barrier(jnp.sum(prejump_sensitivity, axis=0)))
        enc_list.append(jnp.dot(sublevel_entries[reading_depth].T, prejump_sensitivity.astype(jnp.bfloat16), preferred_element_type=jnp.float32).astype(jnp.bfloat16))
        dec_list.append(jnp.stack(dec_rows))
    return (jnp.stack(enc_list), jnp.stack(dec_list), jnp.stack(bias_list))
```

```python
import math

import jax
import jax.numpy as jnp
from jax import lax
from jax.sharding import PartitionSpec as P

BF = jnp.bfloat16
F32 = jnp.float32


def plain_shards(entries, readin, offset, cutoff, writeout, hidden, depth):
    layer = lax.axis_index("layer")
    owner = jnp.logical_and(layer == 0, lax.axis_index("feat") == 0).astype(F32)
    gathered = lax.all_gather(entries, "tok", axis=1, tiled=True)[0]
    inverse = 1.0 / math.sqrt(gathered.shape[0])
    gate = cutoff[0].astype(F32)
    pre = jnp.dot(gathered, readin[0], preferred_element_type=F32) + offset[0][None, :]
    act = (pre * gate).astype(BF)
    live = (layer <= depth).astype(F32)
    targets = writeout.shape[1]
    partials = jnp.stack(
        [jnp.dot(act, writeout[0, t], preferred_element_type=F32) for t in range(targets)]
    )
    rows = hidden.shape[1]
    start = lax.axis_index("tok") * rows
    current = lax.dynamic_slice_in_dim(partials, start, rows, 1)
    partials = lax.dynamic_update_slice_in_dim(
        partials, current - owner * hidden.astype(F32), start, 1
    )
    summed = lax.psum_scatter(
        partials * live[:, None, None], ("feat", "tok"), scatter_dimension=1, tiled=True
    )
    summed = lax.psum(summed, "layer")
    scaled = lax.all_gather((summed * inverse).astype(BF), ("feat", "tok"), axis=1, tiled=True)
    dec = [
        (jnp.einsum("tf,td->fd", act, scaled[t], preferred_element_type=F32) * live[t]).astype(BF)
        for t in range(targets)
    ]
    sens = sum(
        live[t] * jnp.einsum("td,fd->tf", scaled[t], writeout[0, t], preferred_element_type=F32)
        for t in range(targets)
    )
    pre_grad = sens * gate
    enc = jnp.einsum("td,tf->df", gathered, pre_grad.astype(BF), preferred_element_type=F32)
    return enc.astype(BF)[None], jnp.stack(dec)[None], jnp.sum(pre_grad, axis=0)[None]


def column_chunks(width, count):
    tile = 128 if width % 128 == 0 else 1
    tiles = width // tile
    edges = [tile * ((tiles * k + count - 1) // count) for k in range(count + 1)]
    return [(a, b) for a, b in zip(edges[:-1], edges[1:]) if b > a]


def pick(flag, a, b):
    return jnp.where(flag, a, b)


def paired_shards(sizes, entries, readin, offset, cutoff, writeout, hidden, depth):
    layers, feats, toks = sizes
    layer, feat, tok = (lax.axis_index(a) for a in ("layer", "feat", "tok"))
    side, core = tok // 2, tok % 2

    def to_core(a):
        return lax.ppermute(a, "tok", [(t, t ^ 1) for t in range(toks)])

    def to_side(a):
        return lax.ppermute(a, "tok", [(t, t ^ 2) for t in range(toks)])

    def mixed(first):
        pairs = []
        for f in range(feats):
            for t in range(toks):
                over_side = (t % 2 == 0) == first
                goal = (f, t ^ 2) if over_side else (f ^ 1, t)
                pairs.append((f * toks + t, goal[0] * toks + goal[1]))
        return lambda a: lax.ppermute(a, ("feat", "tok"), pairs)

    to_first, to_second = mixed(True), mixed(False)
    binary = layers & (layers - 1) == 0

    def layer_goal(l, s):
        return l ^ s if binary else (l + s) % layers

    def layer_source(l, s):
        return l ^ s if binary else (l - s) % layers

    def to_layer(a, s):
        return lax.ppermute(a, "layer", [(l, layer_goal(l, s)) for l in range(layers)])

    own = entries[0]
    rows, width = own.shape
    total = rows * toks
    half = total // 2
    inverse = 1.0 / math.sqrt(total)
    live = (layer <= depth).astype(F32)
    weights = writeout[0]

    far = to_side(own)
    near = to_core(own)
    far_near = to_core(far)
    zero_core = core == 0
    tokens = jnp.concatenate(
        [
            pick(zero_core, own, near),
            pick(zero_core, near, own),
            pick(zero_core, far, far_near),
            pick(zero_core, far_near, far),
        ]
    )
    swapped = side == 1
    gate = cutoff[0]
    gate = jnp.concatenate(
        [
            lax.dynamic_slice_in_dim(gate, side * half, half, 0),
            lax.dynamic_slice_in_dim(gate, (1 - side) * half, half, 0),
        ]
    ).astype(F32)
    pre = jnp.dot(tokens, readin[0], preferred_element_type=F32) + offset[0][None, :]
    act = (pre * gate).astype(BF)

    flag = jnp.logical_and(layer == 0, feat == 0).astype(F32)
    mine_hidden = hidden.astype(F32) * flag

    def partial(target, lo, hi):
        w = lax.dynamic_index_in_dim(weights, target, 0, keepdims=False)[:, lo:hi]
        out = jnp.dot(act, w, preferred_element_type=F32).reshape(4, rows, hi - lo)
        sub = lax.dynamic_index_in_dim(mine_hidden, target, 0, keepdims=False)[:, lo:hi]
        place = (jnp.arange(4) == core).astype(F32)[:, None, None]
        return (out - place * sub[None]) * live[target]

    y1 = feat == 1

    def chunk(lo, hi):
        away = partial(1 - core, lo, hi).astype(BF)
        kept = partial(core, lo, hi)
        summed = kept + to_core(away).astype(F32)
        b0, b1, b2, b3 = (summed[i] for i in range(4))
        send = jnp.stack(
            [
                pick(zero_core, b0, pick(y1, b0, b1)),
                pick(zero_core, b1, pick(y1, b2, b3)),
            ]
        ).astype(BF)
        keep = jnp.stack(
            [
                pick(zero_core, b2, pick(y1, b1, b0)),
                pick(zero_core, b3, pick(y1, b3, b2)),
            ]
        )
        pair = keep + to_first(send).astype(F32)
        second = jnp.logical_or(jnp.logical_not(zero_core), y1)
        send = pick(second, pair[0], pair[1]).astype(BF)
        keep = pick(second, pair[1], pair[0])
        block = keep + to_second(send).astype(F32)
        piece = rows // layers
        low = block.astype(BF)
        mine = lax.dynamic_slice_in_dim(block, layer * piece, piece, 0)
        for s in range(1, layers):
            out = lax.dynamic_slice_in_dim(low, layer_goal(layer, s) * piece, piece, 0)
            mine = mine + to_layer(out, s).astype(F32)
        scaled = (mine * inverse).astype(BF)
        done = jnp.zeros((rows, hi - lo), BF)
        done = lax.dynamic_update_slice_in_dim(done, scaled, layer * piece, 0)
        for s in range(1, layers):
            done = lax.dynamic_update_slice_in_dim(
                done, to_layer(scaled, s), layer_source(layer, s) * piece, 0
            )
        got = to_second(done)
        m0, m1 = pick(second, got, done), pick(second, done, got)
        got = to_first(jnp.stack([m0, m1]))
        r0, r1 = got[0], got[1]
        full = jnp.stack(
            [
                pick(zero_core, r0, pick(y1, r0, m0)),
                pick(zero_core, r1, pick(y1, m0, r0)),
                pick(zero_core, m0, pick(y1, r1, m1)),
                pick(zero_core, m1, pick(y1, m1, r1)),
            ]
        ).reshape(total, hi - lo)
        other = to_core(full)
        return pick(zero_core, full, other), pick(zero_core, other, full)

    act_turned = act.T
    tokens_turned = tokens.T
    sens = jnp.zeros(act.shape, F32)
    dec = [[], []]
    for lo, hi in column_chunks(width, CHUNKS):
        for t, scaled in enumerate(chunk(lo, hi)):
            dec[t].append(
                (jnp.dot(act_turned, scaled, preferred_element_type=F32) * live[t]).astype(BF)
            )
            sens = sens + live[t] * jnp.einsum(
                "td,fd->tf", scaled, weights[t, :, lo:hi], preferred_element_type=F32
            )
    pre_grad = sens * gate
    bias = jnp.sum(pre_grad, axis=0)
    enc = jnp.dot(tokens_turned, pre_grad.astype(BF), preferred_element_type=F32).astype(BF)
    dec = jnp.stack([jnp.concatenate(d, axis=1) for d in dec])
    return enc[None], dec[None], bias[None]


CHUNKS = 2


def solution(mesh):
    sizes = tuple(mesh.shape[a] for a in ("layer", "feat", "tok"))

    def shards(*args):
        rows = args[0].shape[1]
        targets = args[4].shape[1]
        if sizes[1] == targets == 2 and sizes[2] == 4 and rows % sizes[0] == 0:
            return paired_shards(sizes, *args)
        return plain_shards(*args)

    return jax.shard_map(
        shards,
        mesh=mesh,
        in_specs=(
            P("layer", "tok", None),
            P("layer", None, ("feat", "tok")),
            P("layer", ("feat", "tok")),
            P("layer", None, ("feat", "tok")),
            P("layer", None, ("feat", "tok"), None),
            P(None, "tok", None),
            P(),
        ),
        out_specs=(
            P("layer", None, ("feat", "tok")),
            P("layer", None, ("feat", "tok"), None),
            P("layer", ("feat", "tok")),
        ),
        check_vma=False,
    )
```

```python
import math

import jax
import jax.numpy as jnp
from jax import lax
from jax.experimental import pallas as pl
from jax.experimental.pallas import tpu as pltpu
from jax.sharding import PartitionSpec as P

BF = jnp.bfloat16
F32 = jnp.float32


def plain_shards(entries, readin, offset, cutoff, writeout, hidden, depth):
    layer = lax.axis_index("layer")
    owner = jnp.logical_and(layer == 0, lax.axis_index("feat") == 0).astype(F32)
    gathered = lax.all_gather(entries, "tok", axis=1, tiled=True)[0]
    inverse = 1.0 / math.sqrt(gathered.shape[0])
    gate = cutoff[0].astype(F32)
    pre = jnp.dot(gathered, readin[0], preferred_element_type=F32) + offset[0][None, :]
    act = (pre * gate).astype(BF)
    live = (layer <= depth).astype(F32)
    targets = writeout.shape[1]
    partials = jnp.stack(
        [jnp.dot(act, writeout[0, t], preferred_element_type=F32) for t in range(targets)]
    )
    rows = hidden.shape[1]
    start = lax.axis_index("tok") * rows
    current = lax.dynamic_slice_in_dim(partials, start, rows, 1)
    partials = lax.dynamic_update_slice_in_dim(
        partials, current - owner * hidden.astype(F32), start, 1
    )
    summed = lax.psum_scatter(
        partials * live[:, None, None], ("feat", "tok"), scatter_dimension=1, tiled=True
    )
    summed = lax.psum(summed, "layer")
    scaled = lax.all_gather((summed * inverse).astype(BF), ("feat", "tok"), axis=1, tiled=True)
    dec = [
        (jnp.einsum("tf,td->fd", act, scaled[t], preferred_element_type=F32) * live[t]).astype(BF)
        for t in range(targets)
    ]
    sens = sum(
        live[t] * jnp.einsum("td,fd->tf", scaled[t], writeout[0, t], preferred_element_type=F32)
        for t in range(targets)
    )
    pre_grad = sens * gate
    enc = jnp.einsum("td,tf->df", gathered, pre_grad.astype(BF), preferred_element_type=F32)
    return enc.astype(BF)[None], jnp.stack(dec)[None], jnp.sum(pre_grad, axis=0)[None]


def column_chunks(width):
    for parts in (3, 2):
        if width % (128 * parts) == 0:
            unit = width // parts
            return [(0, width - unit), (width - unit, width)]
    return [(0, width)]


VMEM_MIB = 16
FEATURE_BLOCK = 256
ROWS_UNIT = 128
SIDE, CORE, FEAT, LAYER = range(4)
HELD = pl.BlockSpec(memory_space=pltpu.VMEM)
ANYWHERE = pl.BlockSpec(memory_space=pl.ANY)


def held(shape, dtype):
    return pltpu.VMEM(shape, dtype)


def array(shape, dtype):
    return jax.ShapeDtypeStruct(shape, dtype)


def block_of(features):
    return FEATURE_BLOCK if features % FEATURE_BLOCK == 0 else features


def span(number, size):
    return pl.ds(pl.multiple_of(number * size, size), size)


class Order:
    def __init__(self, scalars):
        self.scalars = scalars
        self.last = None

    def __call__(
        self, kernel, operands, outs, specs=None, out_specs=None, grid=(1,), scratch=(), aliases=()
    ):
        count = len(operands)
        operands = list(operands)
        specs = list(specs or [HELD] * count)
        waits = [] if self.last is None else [self.last]

        def body(*refs):
            at = len(self.scalars) + count
            kernel(*refs[:at], *refs[at + len(waits) :])

        results = pl.pallas_call(
            body,
            grid_spec=pltpu.PrefetchScalarGridSpec(
                num_scalar_prefetch=len(self.scalars),
                grid=grid,
                in_specs=specs + [ANYWHERE] * len(waits),
                out_specs=list(out_specs or [HELD] * len(outs)),
                scratch_shapes=list(scratch),
            ),
            out_shape=list(outs),
            input_output_aliases={len(self.scalars) + i: o for i, o in aliases},
            compiler_params=pltpu.CompilerParams(vmem_limit_bytes=VMEM_MIB * 1024 * 1024),
            cost_estimate=pl.CostEstimate(flops=1000, bytes_accessed=1000, transcendentals=0),
        )(*self.scalars, *operands, *waits)
        self.last = results[0]
        return results

    def pass_on(self, value):
        def kernel(*refs):
            pass

        last = self.last
        out = self(kernel, [value], [array(value.shape, value.dtype)], [ANYWHERE], [ANYWHERE],
                   aliases=[(0, 0)])[0]
        self.last = last
        return out


def load(order, *operands):
    parts = []
    for k, o in enumerate(operands):
        axis = max(range(o.ndim - 1), key=lambda i: o.shape[i])
        cuts = 4 if o.shape[axis] % 64 == 0 else 1
        size = o.shape[axis] // cuts
        for c in range(cuts):
            parts.append((k, (slice(None),) * axis + (pl.ds(c * size, size),)))

    def kernel(w, d, *refs):
        *refs, sems = refs
        n = len(operands)
        copies = [
            pltpu.make_async_copy(refs[k].at[at], refs[n + k].at[at], sems.at[i])
            for i, (k, at) in enumerate(parts)
        ]
        for copy in copies:
            copy.start()
        for copy in copies:
            copy.wait()

    return order(
        kernel,
        [pltpu.with_memory_space_constraint(o, pltpu.HBM) for o in operands],
        [held(o.shape, o.dtype) for o in operands],
        specs=[pl.BlockSpec(memory_space=pltpu.HBM)] * len(operands),
        scratch=[pltpu.SemaphoreType.DMA((len(parts),))],
    )


def encode(order, near, parts, readin, offset, cutoff):
    rows, width = parts[0].shape
    count = 2 * rows
    features = readin.shape[-1]
    block = block_of(features)

    def kernel(
        w, d, own_ref, other_ref, readin_ref, offset_ref, cutoff_ref, act_ref, turned_ref, tokens_ref
    ):
        i = pl.program_id(0)
        cols = span(i, block)
        first = w[SIDE] if near else 1 - w[SIDE]
        for ref, number in ((own_ref, w[CORE]), (other_ref, 1 - w[CORE])):
            at = span(number, rows)
            pre = jnp.dot(ref[...], readin_ref[0, :, cols], preferred_element_type=F32)
            gate = cutoff_ref[0, span(2 * first + number, rows), cols].astype(F32)
            act = ((pre + offset_ref[:, cols]) * gate).astype(BF)
            act_ref[at, cols] = act
            turned_ref[cols, at] = act.T

            @pl.when(i == 0)
            def _():
                tokens_ref[:, at] = ref[...].T

    return order(
        kernel,
        [*parts, readin, offset, cutoff],
        [held((count, features), BF), held((features, count), BF), held((width, count), BF)],
        grid=(features // block,),
    )


def decode(order, away, act, writeout, hidden, lo, hi, unit):
    count, features = act.shape
    dtype = BF if away else F32

    def kernel(w, d, act_ref, weight_ref, *rest):
        out_ref = rest[-1]
        target = 1 - w[CORE] if away else w[CORE]
        live = jnp.where(w[LAYER] <= d[target], 1.0, 0.0)
        owner = jnp.logical_and(w[LAYER] == 0, w[FEAT] == 0)
        for j in range(lo, hi, unit):
            cols, to = slice(j, j + unit), slice(j - lo, j - lo + unit)
            out = jnp.dot(act_ref[...], weight_ref[0, target, :, cols], preferred_element_type=F32)
            if hidden is None:
                out_ref[:, to] = (out * live).astype(dtype)
                continue
            less = rest[0][target, :, cols].astype(F32)
            rows = less.shape[0]
            for b in range(count // rows):
                mine = jnp.where(jnp.logical_and(owner, w[CORE] == b), 1.0, 0.0)
                part = out[b * rows : (b + 1) * rows] - mine * less
                out_ref[b * rows : (b + 1) * rows, to] = (part * live).astype(dtype)

    operands = [act, writeout] + ([] if hidden is None else [hidden])
    return order(kernel, operands, [held((count, hi - lo), dtype)])[0]


def gradients(order, scaled, turned, writeout, lo, hi, sens=None, dec=None, last=None):
    targets, features, width = writeout.shape[1:]
    total, columns = scaled[0].shape
    count = turned[0].shape[1]
    block = block_of(features)
    at = lo // columns

    def kernel(w, d, *refs):
        refs = list(refs)
        s_refs = [refs.pop(0) for _ in range(targets)]
        near_ref, far_ref, weight_ref = refs.pop(0), refs.pop(0), refs.pop(0)
        sens_in = refs.pop(0) if sens is not None else None
        if last is not None:
            cutoff_ref, token_refs = refs.pop(0), [refs.pop(0), refs.pop(0)]
        if dec is not None:
            refs.pop(0)
        dec_ref = refs.pop(0)
        cols = span(pl.program_id(0), block)
        numbers = [w[CORE], 1 - w[CORE]]
        live = [jnp.where(w[LAYER] <= d[n], 1.0, 0.0) for n in numbers]
        grads = [None, None]
        for half in range(2):
            rows = slice(half * count, (half + 1) * count)
            grad = 0.0 if sens_in is None else sens_in[rows, cols]
            for t in range(targets):
                grad = grad + live[t] * lax.dot_general(
                    s_refs[t][rows, :],
                    weight_ref[0, numbers[t], cols, lo:hi],
                    (((1,), (1,)), ((), ())),
                    preferred_element_type=F32,
                )
            grads[half] = grad
        if last is None:
            for half in range(2):
                refs[0][half * count : (half + 1) * count, cols] = grads[half]
        else:
            enc_ref, bias_ref = refs
            sides = [w[SIDE], 1 - w[SIDE]]
            grads = [
                g * cutoff_ref[0, span(s, count), cols].astype(F32) for g, s in zip(grads, sides)
            ]
            bias_ref[...] = sum(jnp.sum(g, axis=0, keepdims=True) for g in grads)
            enc_ref[0] = sum(
                jnp.dot(ref[...], g.astype(BF), preferred_element_type=F32)
                for ref, g in zip(token_refs, grads)
            ).astype(BF)
        for t in range(targets):
            out = jnp.dot(near_ref[cols, :], s_refs[t][:count, :], preferred_element_type=F32)
            out += jnp.dot(far_ref[cols, :], s_refs[t][count:, :], preferred_element_type=F32)
            dec_ref[0, numbers[t]] = (out * live[t]).astype(BF)

    operands = [*scaled, *turned, writeout]
    if sens is not None:
        operands.append(sens)
    if last is not None:
        operands += [last[0], *last[1]]
    specs = [HELD] * len(operands)
    aliases = []
    if dec is not None:
        aliases = [(len(operands), 0)]
        operands.append(dec)
        specs.append(ANYWHERE)
    out_specs = [pl.BlockSpec((1, targets, block, columns), lambda i, w, d: (0, 0, i, at))]
    outs = [array(writeout.shape, BF)]
    if last is not None:
        out_specs.append(pl.BlockSpec((1, width, block), lambda i, w, d: (0, 0, i)))
        out_specs.append(pl.BlockSpec((1, block), lambda i, w, d: (0, i)))
        outs += [array((1, width, features), BF), array((1, features), F32)]
    else:
        out_specs.append(HELD)
        outs.append(held((total, features), F32))
    results = order(
        kernel, operands, outs, specs, out_specs, grid=(features // block,), aliases=aliases
    )
    if last is None:
        order.last = results[1]
    return results


def paired_shards(sizes, entries, readin, offset, cutoff, writeout, hidden, depth):
    layers, feats, toks = sizes
    layer, feat, tok = (lax.axis_index(a) for a in ("layer", "feat", "tok"))
    where = jnp.stack([tok // 2, tok % 2, feat, layer]).astype(jnp.int32)
    order = Order((where, depth))

    def to_core(a):
        return lax.ppermute(a, "tok", [(t, t ^ 1) for t in range(toks)])

    def to_side(a):
        return lax.ppermute(a, "tok", [(t, t ^ 2) for t in range(toks)])

    def mixed(first):
        pairs = []
        for f in range(feats):
            for t in range(toks):
                over_side = (t % 2 == 0) == first
                goal = (f, t ^ 2) if over_side else (f ^ 1, t)
                pairs.append((f * toks + t, goal[0] * toks + goal[1]))
        return lambda a: lax.ppermute(a, ("feat", "tok"), pairs)

    to_first, to_second = mixed(True), mixed(False)
    binary = layers & (layers - 1) == 0

    def layer_goal(l, s):
        return l ^ s if binary else lax.rem(l + s, layers)

    def layer_source(l, s):
        return l ^ s if binary else lax.rem(l - s + layers, layers)

    def to_layer(a, s):
        return lax.ppermute(
            a, "layer", [(l, l ^ s if binary else (l + s) % layers) for l in range(layers)]
        )

    own = entries[0]
    rows, width = own.shape
    total = rows * toks
    inverse = 1.0 / math.sqrt(total)
    piece = rows // layers
    chunks = column_chunks(width)
    unit = chunks[-1][1] - chunks[-1][0]

    far = to_side(own)
    near = to_core(own)
    readin, cutoff, writeout, hidden = load(order, readin, cutoff, writeout, hidden)
    act, turned, tokens = encode(order, True, (own, near), readin, offset, cutoff)

    def partials(act, hidden, lo, hi):
        away = decode(order, True, act, writeout, hidden, lo, hi, unit)
        got = to_core(away)
        return decode(order, False, act, writeout, hidden, lo, hi, unit), got

    here = partials(act, hidden, 0, width)

    def first_kernel(w, d, kept, got, out):
        at = span(1 - w[FEAT], rows)
        out[...] = (kept[at, :] + got[at, :].astype(F32)).astype(BF)

    send = order(first_kernel, here, [held((rows, width), BF)])[0]
    got_first = to_first(send)

    far = order.pass_on(far)
    far_near = to_core(far)
    act, turned_far, tokens_far = encode(order, False, (far, far_near), readin, offset, cutoff)

    def reduce_sides(lo, hi):
        size = hi - lo
        there = partials(act, None, lo, hi)

        def second_kernel(w, d, hk, hg, tk, tg, first, out_first, out_second):
            at, other = span(w[FEAT], rows), span(1 - w[FEAT], rows)
            here_y = hk[at, lo:hi] + hg[at, lo:hi].astype(F32)
            there_other = tk[other, :] + tg[other, :].astype(F32)
            zero = w[CORE] == 0
            out_first[...] = jnp.where(zero, here_y, there_other).astype(BF)
            rest = jnp.where(zero, there_other, here_y) + first[:, lo:hi].astype(F32)
            out_second[...] = rest.astype(BF)

        sends = order(second_kernel, (*here, *there, got_first), [held((rows, size), BF)] * 2)
        return there, to_first(sends[0]), to_second(sends[1])

    def send_pieces(there, got, got_second):
        size = got.shape[1]

        def kernel(w, d, tk, tg, first, second, mine, *outs):
            *outs, kept = outs
            at = span(w[FEAT], rows)
            kept[...] = (
                tk[at, :]
                + tg[at, :].astype(F32)
                + first[...].astype(F32)
                + second[...].astype(F32)
            )
            mine[...] = kept[span(w[LAYER], piece), :]
            for s, out in enumerate(outs, 1):
                out[...] = kept[span(layer_goal(w[LAYER], s), piece), :].astype(BF)

        outs = [held((piece, size), F32)] + [held((piece, size), BF)] * (layers - 1)
        mine, *outs = order(
            kernel, (*there, got, got_second), outs, scratch=[pltpu.VMEM((rows, size), F32)]
        )
        return mine, [to_layer(out, s) for s, out in enumerate(outs, 1)]

    def scale_piece(mine, pieces):
        def kernel(w, d, mine_ref, *refs):
            *refs, out = refs
            value = mine_ref[...]
            for ref in refs:
                value = value + ref[...].astype(F32)
            out[...] = (value * inverse).astype(BF)

        scaled = order(kernel, (mine, *pieces), [held(mine.shape, BF)])[0]
        return scaled, [to_layer(scaled, s) for s in range(1, layers)]

    def join_pieces(scaled, pieces):
        def kernel(w, d, *refs):
            *refs, out = refs
            out[span(w[LAYER], piece), :] = refs[0][...]
            for s, ref in enumerate(refs[1:], 1):
                out[span(layer_source(w[LAYER], s), piece), :] = ref[...]

        done = order(kernel, (scaled, *pieces), [held((rows, scaled.shape[1]), BF)])[0]
        return done, to_second(done)

    def join_pair(done, got):
        def kernel(w, d, done_ref, got_ref, out):
            number = jnp.where(w[CORE] == 0, w[FEAT], 1)
            out[span(number, rows), :] = done_ref[...]
            out[span(1 - number, rows), :] = got_ref[...]

        pair = order(kernel, (done, got), [held((2 * rows, done.shape[1]), BF)])[0]
        return pair, to_first(pair)

    def join_all(pair, got):
        def kernel(w, d, pair_ref, got_ref, out):
            zero = w[CORE] == 0
            y = w[FEAT]
            for ref, numbers in (
                (pair_ref, (jnp.where(zero, 2, y), jnp.where(zero, 3, 2 + y))),
                (got_ref, (jnp.where(zero, 0, 1 - y), jnp.where(zero, 1, 3 - y))),
            ):
                for b, number in enumerate(numbers):
                    out[span(number, rows), :] = ref[b * rows : (b + 1) * rows, :]

        full = order(kernel, (pair, got), [held((total, pair.shape[1]), BF)])[0]
        return full, to_core(full)

    stages = [reduce_sides(lo, hi) for lo, hi in chunks]
    stages = [send_pieces(*stage) for stage in stages]
    stages = [scale_piece(*stage) for stage in stages]
    stages = [join_pair(*join_pieces(*stage)) for stage in stages]
    sens = dec = None
    for k, (lo, hi) in enumerate(chunks):
        last = (cutoff, (tokens, tokens_far)) if k == len(chunks) - 1 else None
        scaled = join_all(*stages[k])
        dec, *rest = gradients(
            order, scaled, (turned, turned_far), writeout, lo, hi, sens, dec, last
        )
        sens = rest[0]
    return rest[0], dec, rest[1]


def solution(mesh):
    sizes = tuple(mesh.shape[a] for a in ("layer", "feat", "tok"))

    def shards(*args):
        rows = args[0].shape[1]
        targets = args[4].shape[1]
        paired = sizes[1] == targets == 2 and sizes[2] == 4
        if paired and rows % ROWS_UNIT == 0 and rows % (16 * sizes[0]) == 0:
            return paired_shards(sizes, *args)
        return plain_shards(*args)

    return jax.shard_map(
        shards,
        mesh=mesh,
        in_specs=(
            P("layer", "tok", None),
            P("layer", None, ("feat", "tok")),
            P("layer", ("feat", "tok")),
            P("layer", None, ("feat", "tok")),
            P("layer", None, ("feat", "tok"), None),
            P(None, "tok", None),
            P(),
        ),
        out_specs=(
            P("layer", None, ("feat", "tok")),
            P("layer", None, ("feat", "tok"), None),
            P("layer", ("feat", "tok")),
        ),
        check_vma=False,
    )
```

```python
import math

import jax
import jax.numpy as jnp
from jax import lax
from jax.experimental import pallas as pl
from jax.experimental.pallas import tpu as pltpu
from jax.sharding import PartitionSpec as P

BF = jnp.bfloat16
F32 = jnp.float32


def plain_shards(entries, readin, offset, cutoff, writeout, hidden, depth):
    layer = lax.axis_index("layer")
    owner = jnp.logical_and(layer == 0, lax.axis_index("feat") == 0).astype(F32)
    gathered = lax.all_gather(entries, "tok", axis=1, tiled=True)[0]
    inverse = 1.0 / math.sqrt(gathered.shape[0])
    gate = cutoff[0].astype(F32)
    pre = jnp.dot(gathered, readin[0], preferred_element_type=F32) + offset[0][None, :]
    act = (pre * gate).astype(BF)
    live = (layer <= depth).astype(F32)
    targets = writeout.shape[1]
    partials = jnp.stack(
        [jnp.dot(act, writeout[0, t], preferred_element_type=F32) for t in range(targets)]
    )
    rows = hidden.shape[1]
    start = lax.axis_index("tok") * rows
    current = lax.dynamic_slice_in_dim(partials, start, rows, 1)
    partials = lax.dynamic_update_slice_in_dim(
        partials, current - owner * hidden.astype(F32), start, 1
    )
    summed = lax.psum_scatter(
        partials * live[:, None, None], ("feat", "tok"), scatter_dimension=1, tiled=True
    )
    summed = lax.psum(summed, "layer")
    scaled = lax.all_gather((summed * inverse).astype(BF), ("feat", "tok"), axis=1, tiled=True)
    dec = [
        (jnp.einsum("tf,td->fd", act, scaled[t], preferred_element_type=F32) * live[t]).astype(BF)
        for t in range(targets)
    ]
    sens = sum(
        live[t] * jnp.einsum("td,fd->tf", scaled[t], writeout[0, t], preferred_element_type=F32)
        for t in range(targets)
    )
    pre_grad = sens * gate
    enc = jnp.einsum("td,tf->df", gathered, pre_grad.astype(BF), preferred_element_type=F32)
    return enc.astype(BF)[None], jnp.stack(dec)[None], jnp.sum(pre_grad, axis=0)[None]


def column_chunks(width):
    for parts in (3, 2):
        if width % (128 * parts) == 0:
            unit = width // parts
            return [(0, width - unit), (width - unit, width)]
    return [(0, width)]


VMEM_MIB = 16
FEATURE_BLOCK = 512
ROWS_UNIT = 128
SIDE, CORE, FEAT, LAYER = range(4)
HELD = pl.BlockSpec(memory_space=pltpu.VMEM)
ANYWHERE = pl.BlockSpec(memory_space=pl.ANY)


def held(shape, dtype):
    return pltpu.VMEM(shape, dtype)


def array(shape, dtype):
    return jax.ShapeDtypeStruct(shape, dtype)


def block_of(features):
    return FEATURE_BLOCK if features % FEATURE_BLOCK == 0 else features


def span(number, size):
    return pl.ds(pl.multiple_of(number * size, size), size)


class Order:
    def __init__(self, scalars):
        self.scalars = scalars
        self.last = None

    def __call__(
        self, kernel, operands, outs, specs=None, out_specs=None, grid=(1,), scratch=(), aliases=()
    ):
        count = len(operands)
        operands = list(operands)
        specs = list(specs or [HELD] * count)
        waits = [] if self.last is None else [self.last]

        def body(*refs):
            at = len(self.scalars) + count
            kernel(*refs[:at], *refs[at + len(waits) :])

        results = pl.pallas_call(
            body,
            grid_spec=pltpu.PrefetchScalarGridSpec(
                num_scalar_prefetch=len(self.scalars),
                grid=grid,
                in_specs=specs + [ANYWHERE] * len(waits),
                out_specs=list(out_specs or [HELD] * len(outs)),
                scratch_shapes=list(scratch),
            ),
            out_shape=list(outs),
            input_output_aliases={len(self.scalars) + i: o for i, o in aliases},
            compiler_params=pltpu.CompilerParams(vmem_limit_bytes=VMEM_MIB * 1024 * 1024),
            cost_estimate=pl.CostEstimate(flops=1000, bytes_accessed=1000, transcendentals=0),
        )(*self.scalars, *operands, *waits)
        self.last = results[0]
        return results

    def pass_on(self, value):
        def kernel(*refs):
            pass

        like = array(value.shape, value.dtype)
        return self(kernel, [value], [like], [ANYWHERE], [ANYWHERE], aliases=[(0, 0)])[0]


def load(order, *operands):
    parts = []
    for k, o in enumerate(operands):
        axis = max(range(o.ndim - 1), key=lambda i: o.shape[i])
        cuts = 4 if o.shape[axis] % 64 == 0 else 1
        size = o.shape[axis] // cuts
        for c in range(cuts):
            parts.append((k, (slice(None),) * axis + (pl.ds(c * size, size),)))

    def kernel(w, d, *refs):
        *refs, sems = refs
        n = len(operands)
        copies = [
            pltpu.make_async_copy(refs[k].at[at], refs[n + k].at[at], sems.at[i])
            for i, (k, at) in enumerate(parts)
        ]
        for copy in copies:
            copy.start()
        for copy in copies:
            copy.wait()

    return order(
        kernel,
        [pltpu.with_memory_space_constraint(o, pltpu.HBM) for o in operands],
        [held(o.shape, o.dtype) for o in operands],
        specs=[pl.BlockSpec(memory_space=pltpu.HBM)] * len(operands),
        scratch=[pltpu.SemaphoreType.DMA((len(parts),))],
    )


def encode(order, near, parts, readin, offset, cutoff):
    rows, width = parts[0].shape
    count = 2 * rows

    def kernel(w, d, own_ref, other_ref, readin_ref, offset_ref, cutoff_ref, act_ref, both):
        for ref, number in ((own_ref, w[CORE]), (other_ref, 1 - w[CORE])):
            both[span(number, rows), :] = ref[...]
        first = w[SIDE] if near else 1 - w[SIDE]
        pre = jnp.dot(both[...], readin_ref[0], preferred_element_type=F32)
        gate = cutoff_ref[0, span(first, count), :].astype(F32)
        act_ref[...] = ((pre + offset_ref[...]) * gate).astype(BF)

    return order(
        kernel,
        [*parts, readin, offset, cutoff],
        [held((count, readin.shape[-1]), BF)],
        scratch=[pltpu.VMEM((count, width), BF)],
    )[0]


def turn(order, acts, parts):
    count, features = acts[0].shape
    rows, width = parts[0][0].shape

    def kernel(w, d, *refs):
        act_refs, part_refs, (turned_ref, tokens_ref) = refs[:2], refs[2:6], refs[6:]
        for half in range(2):
            turned_ref[:, half * count : (half + 1) * count] = act_refs[half][...].T
            for ref, number in zip(part_refs[2 * half : 2 * half + 2], (w[CORE], 1 - w[CORE])):
                tokens_ref[:, span(2 * half + number, rows)] = ref[...].T

    return order(
        kernel,
        [*acts, *parts[0], *parts[1]],
        [held((features, 2 * count), BF), held((width, 2 * count), BF)],
    )


def decode(order, away, act, writeout, hidden, lo, hi):
    count, features = act.shape
    blocks = 2
    rows = count // blocks
    dtype = BF if away else F32

    def kernel(w, d, act_ref, weight_ref, *rest):
        target = 1 - w[CORE] if away else w[CORE]
        live = jnp.where(w[LAYER] <= d[target], 1.0, 0.0)
        out = jnp.dot(act_ref[...], weight_ref[0, target, :, lo:hi], preferred_element_type=F32)
        parts = [out[b * rows : (b + 1) * rows] for b in range(blocks)]
        if hidden is not None:
            less = rest[0][target, :, lo:hi].astype(F32)
            owner = jnp.logical_and(w[LAYER] == 0, w[FEAT] == 0)
            mine = [jnp.logical_and(owner, w[CORE] == b) for b in range(blocks)]
            parts = [p - jnp.where(m, 1.0, 0.0) * less for p, m in zip(parts, mine)]
        for ref, part in zip(rest[-blocks:], parts):
            ref[...] = (part * live).astype(dtype)

    operands = [act, writeout] + ([] if hidden is None else [hidden])
    return order(kernel, operands, [held((rows, hi - lo), dtype)] * blocks)


def gradients(order, scaled, turned, writeout, lo, hi, sens=None, dec=None, last=None):
    targets, features, width = writeout.shape[1:]
    total, columns = scaled[0].shape
    count = total // 2
    block = block_of(features)
    at = lo // columns

    def kernel(w, d, *refs):
        refs = list(refs)
        s_refs = [refs.pop(0) for _ in range(targets)]
        turned_ref, weight_ref = refs.pop(0), refs.pop(0)
        sens_in = refs.pop(0) if sens is not None else None
        if last is not None:
            cutoff_ref, tokens_ref = refs.pop(0), refs.pop(0)
        if dec is not None:
            refs.pop(0)
        dec_ref = refs.pop(0)
        cols = span(pl.program_id(0), block)
        numbers = [w[CORE], 1 - w[CORE]]
        grad = 0.0 if sens_in is None else sens_in[:, cols]
        for ref, number in zip(s_refs, numbers):
            grad = grad + lax.dot_general(
                ref[...],
                weight_ref[0, number, cols, lo:hi],
                (((1,), (1,)), ((), ())),
                preferred_element_type=F32,
            )
        if last is None:
            refs[0][:, cols] = grad
        else:
            enc_ref, bias_ref, low_ref = refs
            biases = 0.0
            for half, side in enumerate((w[SIDE], 1 - w[SIDE])):
                rows = slice(half * count, (half + 1) * count)
                part = grad[rows] * cutoff_ref[0, span(side, count), cols].astype(F32)
                biases = biases + jnp.sum(part, axis=0, keepdims=True)
                low_ref[rows, :] = part.astype(BF)
            bias_ref[...] = biases
            enc_ref[0] = jnp.dot(
                tokens_ref[...], low_ref[...], preferred_element_type=F32
            ).astype(BF)
        for ref, number in zip(s_refs, numbers):
            out = jnp.dot(turned_ref[cols, :], ref[...], preferred_element_type=F32)
            dec_ref[0, number] = out.astype(BF)

    operands = [*scaled, turned, writeout]
    if sens is not None:
        operands.append(sens)
    if last is not None:
        operands += last
    specs = [HELD] * len(operands)
    aliases = []
    if dec is not None:
        aliases = [(len(operands), 0)]
        operands.append(dec)
        specs.append(ANYWHERE)
    out_specs = [pl.BlockSpec((1, targets, block, columns), lambda i, w, d: (0, 0, i, at))]
    outs = [array(writeout.shape, BF)]
    scratch = []
    if last is not None:
        out_specs.append(pl.BlockSpec((1, width, block), lambda i, w, d: (0, 0, i)))
        out_specs.append(pl.BlockSpec((1, block), lambda i, w, d: (0, i)))
        outs += [array((1, width, features), BF), array((1, features), F32)]
        scratch.append(pltpu.VMEM((total, block), BF))
    else:
        out_specs.append(HELD)
        outs.append(held((total, features), F32))
    results = order(
        kernel, operands, outs, specs, out_specs, (features // block,), scratch, aliases
    )
    if last is None:
        order.last = results[1]
    return results


def pick(flag, a, b):
    return jnp.where(flag, a, b)


def paired_shards(sizes, entries, readin, offset, cutoff, writeout, hidden, depth):
    layers, feats, toks = sizes
    layer, feat, tok = (lax.axis_index(a) for a in ("layer", "feat", "tok"))
    where = jnp.stack([tok // 2, tok % 2, feat, layer]).astype(jnp.int32)
    order = Order((where, depth))

    def to_core(a):
        return lax.ppermute(a, "tok", [(t, t ^ 1) for t in range(toks)])

    def to_side(a):
        return lax.ppermute(a, "tok", [(t, t ^ 2) for t in range(toks)])

    def mixed(first):
        pairs = []
        for f in range(feats):
            for t in range(toks):
                over_side = (t % 2 == 0) == first
                goal = (f, t ^ 2) if over_side else (f ^ 1, t)
                pairs.append((f * toks + t, goal[0] * toks + goal[1]))
        return lambda a: lax.ppermute(a, ("feat", "tok"), pairs)

    to_first, to_second = mixed(True), mixed(False)
    binary = layers & (layers - 1) == 0

    def layer_goal(l, s):
        return l ^ s if binary else lax.rem(l + s, layers)

    def layer_source(l, s):
        return l ^ s if binary else lax.rem(l - s + layers, layers)

    def to_layer(a, s):
        return lax.ppermute(
            a, "layer", [(l, l ^ s if binary else (l + s) % layers) for l in range(layers)]
        )

    own = entries[0]
    rows, width = own.shape
    total = rows * toks
    inverse = 1.0 / math.sqrt(total)
    piece = rows // layers
    chunks = column_chunks(width)

    far = to_side(own)
    near = to_core(own)
    readin, cutoff, writeout, hidden = load(order, readin, cutoff, writeout, hidden)
    act_near = encode(order, True, (own, near), readin, offset, cutoff)

    def partials(act, hidden, lo, hi):
        away = decode(order, True, act, writeout, hidden, lo, hi)
        got = [to_core(a) for a in away]
        return (*decode(order, False, act, writeout, hidden, lo, hi), *got)

    here = partials(act_near, hidden, 0, width)
    far = order.pass_on(far)

    def first_kernel(w, d, kept0, kept1, got0, got1, out):
        other = pick(w[FEAT] == 1, kept0[...], kept1[...])
        out[...] = (other + pick(w[FEAT] == 1, got0[...], got1[...]).astype(F32)).astype(BF)

    send = order(first_kernel, here, [held((rows, width), BF)])[0]
    got_first = to_first(send)

    far_near = to_core(far)
    act_far = encode(order, False, (far, far_near), readin, offset, cutoff)

    def reduce_sides(lo, hi):
        size = hi - lo
        there = partials(act_far, None, lo, hi)

        def second_kernel(
            w, d, hk0, hk1, hg0, hg1, tk0, tk1, tg0, tg1, first, out_first, out_second
        ):
            y0 = w[FEAT] == 0
            here_y = pick(y0, hk0[:, lo:hi], hk1[:, lo:hi])
            here_y += pick(y0, hg0[:, lo:hi], hg1[:, lo:hi]).astype(F32)
            there_other = pick(y0, tk1[...], tk0[...])
            there_other += pick(y0, tg1[...], tg0[...]).astype(F32)
            zero = w[CORE] == 0
            out_first[...] = pick(zero, here_y, there_other).astype(BF)
            rest = pick(zero, there_other, here_y) + first[:, lo:hi].astype(F32)
            out_second[...] = rest.astype(BF)

        sends = order(second_kernel, (*here, *there, got_first), [held((rows, size), BF)] * 2)
        return there, to_first(sends[0]), to_second(sends[1])

    def exchange(previous, reduced):
        ahead = 0 if previous is None else previous[0].shape[1]
        behind = 0 if previous is None else previous[1][0].shape[1] - ahead
        size = 0 if reduced is None else reduced[2].shape[1]

        def kernel(w, d, *refs):
            refs = list(refs)
            if previous is not None:
                value = refs.pop(0)[...]
                for _ in previous[1]:
                    value = value + refs.pop(0)[:, behind:].astype(F32)
                value = (value * inverse).astype(BF)
            if reduced is not None:
                tk0, tk1, tg0, tg1, first, second = (refs.pop(0) for _ in range(6))
                kept = refs.pop()
                y0 = w[FEAT] == 0
                kept[...] = (
                    pick(y0, tk0[...], tk1[...])
                    + pick(y0, tg0[...], tg1[...]).astype(F32)
                    + first[...].astype(F32)
                    + second[...].astype(F32)
                )
            if previous is not None:
                refs.pop(0)[...] = value
            if reduced is not None:
                refs.pop(0)[...] = kept[span(w[LAYER], piece), :]
            for s, out in enumerate(refs, 1):
                if previous is not None:
                    out[:, :ahead] = value
                if reduced is not None:
                    goal = layer_goal(w[LAYER], s)
                    out[:, ahead:] = kept[span(goal, piece), :].astype(BF)

        operands, outs, scratch = [], [], []
        if previous is not None:
            operands += [previous[0], *previous[1]]
            outs.append(held((piece, ahead), BF))
        if reduced is not None:
            there, got, got_second = reduced
            operands += [*there, got, got_second]
            outs.append(held((piece, size), F32))
            scratch.append(pltpu.VMEM((rows, size), F32))
        mine = len(outs)
        outs += [held((piece, ahead + size), BF)] * (layers - 1)
        results = order(kernel, operands, outs, scratch=scratch)
        came = [to_layer(out, s) for s, out in enumerate(results[mine:], 1)]
        scaled = None if previous is None else results[0]
        return scaled, None if reduced is None else results[mine - 1], came

    def join_pieces(scaled, pieces):
        size = scaled.shape[1]

        def kernel(w, d, *refs):
            *refs, out = refs
            out[span(w[LAYER], piece), :] = refs[0][...]
            for s, ref in enumerate(refs[1:], 1):
                out[span(layer_source(w[LAYER], s), piece), :] = ref[:, :size]

        done = order(kernel, (scaled, *pieces), [held((rows, size), BF)])[0]
        return done, to_second(done)

    def join_pair(done, got):
        def kernel(w, d, done_ref, got_ref, out0, out1):
            done_last = jnp.logical_or(w[CORE] == 1, w[FEAT] == 1)
            out0[...] = pick(done_last, got_ref[...], done_ref[...])
            out1[...] = pick(done_last, done_ref[...], got_ref[...])

        pair = order(kernel, (done, got), [held(done.shape, BF)] * 2)
        return pair, [to_first(block) for block in pair]

    def join_all(pair, got):
        def kernel(w, d, pair0, pair1, got0, got1, out):
            zero = w[CORE] == 0
            y = w[FEAT]
            live = jnp.where(w[LAYER] <= d[w[CORE]], 1.0, 0.0).astype(BF)
            for ref, number in (
                (pair0, pick(zero, 2, y)),
                (pair1, pick(zero, 3, 2 + y)),
                (got0, pick(zero, 0, 1 - y)),
                (got1, pick(zero, 1, 3 - y)),
            ):
                out[span(number, rows), :] = ref[...] * live

        size = pair[0].shape[1]
        full = order(kernel, (*pair, *got), [held((total, size), BF)])[0]
        return full, to_core(full)

    reduced = [reduce_sides(lo, hi) for lo, hi in chunks]
    turned, tokens = turn(order, (act_near, act_far), ((own, near), (far, far_near)))
    scaled, mine, came = exchange(None, reduced[0])
    pairs = []
    joined = None
    for k in range(len(chunks)):
        scaled, mine, then = exchange((mine, came), (reduced + [None])[k + 1])
        if joined is not None:
            pairs.append(join_pair(*joined))
        came = then
        joined = join_pieces(scaled, came)
    pairs.append(join_pair(*joined))
    scaled = [join_all(*pair) for pair in pairs]
    sens = dec = None
    for k, (lo, hi) in enumerate(chunks):
        last = (cutoff, tokens) if k == len(chunks) - 1 else None
        dec, *rest = gradients(order, scaled[k], turned, writeout, lo, hi, sens, dec, last)
        sens = rest[0]
    return rest[0], dec, rest[1]


def solution(mesh):
    sizes = tuple(mesh.shape[a] for a in ("layer", "feat", "tok"))

    def shards(*args):
        rows = args[0].shape[1]
        targets = args[4].shape[1]
        paired = sizes[1] == targets == 2 and sizes[2] == 4
        if paired and rows % ROWS_UNIT == 0 and rows % (16 * sizes[0]) == 0:
            return paired_shards(sizes, *args)
        return plain_shards(*args)

    return jax.shard_map(
        shards,
        mesh=mesh,
        in_specs=(
            P("layer", "tok", None),
            P("layer", None, ("feat", "tok")),
            P("layer", ("feat", "tok")),
            P("layer", None, ("feat", "tok")),
            P("layer", None, ("feat", "tok"), None),
            P(None, "tok", None),
            P(),
        ),
        out_specs=(
            P("layer", None, ("feat", "tok")),
            P("layer", None, ("feat", "tok"), None),
            P("layer", ("feat", "tok")),
        ),
        check_vma=False,
    )
```

```python
import math

import jax
import jax.numpy as jnp
from jax import lax
from jax.experimental import pallas as pl
from jax.experimental.pallas import tpu as pltpu
from jax.sharding import PartitionSpec as P

BF = jnp.bfloat16
F32 = jnp.float32


def plain_shards(entries, readin, offset, cutoff, writeout, hidden, depth):
    layer = lax.axis_index("layer")
    owner = jnp.logical_and(layer == 0, lax.axis_index("feat") == 0).astype(F32)
    gathered = lax.all_gather(entries, "tok", axis=1, tiled=True)[0]
    inverse = 1.0 / math.sqrt(gathered.shape[0])
    gate = cutoff[0].astype(F32)
    pre = jnp.dot(gathered, readin[0], preferred_element_type=F32) + offset[0][None, :]
    act = (pre * gate).astype(BF)
    live = (layer <= depth).astype(F32)
    targets = writeout.shape[1]
    partials = jnp.stack(
        [jnp.dot(act, writeout[0, t], preferred_element_type=F32) for t in range(targets)]
    )
    rows = hidden.shape[1]
    start = lax.axis_index("tok") * rows
    current = lax.dynamic_slice_in_dim(partials, start, rows, 1)
    partials = lax.dynamic_update_slice_in_dim(
        partials, current - owner * hidden.astype(F32), start, 1
    )
    summed = lax.psum_scatter(
        partials * live[:, None, None], ("feat", "tok"), scatter_dimension=1, tiled=True
    )
    summed = lax.psum(summed, "layer")
    scaled = lax.all_gather((summed * inverse).astype(BF), ("feat", "tok"), axis=1, tiled=True)
    dec = [
        (jnp.einsum("tf,td->fd", act, scaled[t], preferred_element_type=F32) * live[t]).astype(BF)
        for t in range(targets)
    ]
    sens = sum(
        live[t] * jnp.einsum("td,fd->tf", scaled[t], writeout[0, t], preferred_element_type=F32)
        for t in range(targets)
    )
    pre_grad = sens * gate
    enc = jnp.einsum("td,tf->df", gathered, pre_grad.astype(BF), preferred_element_type=F32)
    return enc.astype(BF)[None], jnp.stack(dec)[None], jnp.sum(pre_grad, axis=0)[None]


def column_chunks(width):
    for parts in (3, 2):
        if width % (128 * parts) == 0:
            unit = width // parts
            return [(0, width - unit), (width - unit, width)]
    return [(0, width)]


VMEM_MIB = 16
FEATURE_BLOCK = 512
ROWS_UNIT = 128
HEAVY = 10**11
SIDE, CORE, FEAT, LAYER = range(4)
HELD = pl.BlockSpec(memory_space=pltpu.VMEM)
ANYWHERE = pl.BlockSpec(memory_space=pl.ANY)


def held(shape, dtype):
    return pltpu.VMEM(shape, dtype)


def array(shape, dtype):
    return jax.ShapeDtypeStruct(shape, dtype)


def block_of(features):
    return FEATURE_BLOCK if features % FEATURE_BLOCK == 0 else features


def span(number, size):
    return pl.ds(pl.multiple_of(number * size, size), size)


class Order:
    def __init__(self, scalars):
        self.scalars = scalars
        self.last = None
        self.keep = []

    def __call__(
        self,
        kernel,
        operands,
        outs,
        specs=None,
        out_specs=None,
        grid=(1,),
        scratch=(),
        aliases=(),
        heavy=False,
    ):
        count = len(operands)
        operands = list(operands)
        specs = list(specs or [HELD] * count)
        waits = [] if self.last is None else [self.last]
        keep = [k for k in self.keep if all(k is not o for o in operands)]

        def body(*refs):
            at = len(self.scalars) + count
            kernel(*refs[:at], *refs[at + len(waits) + len(keep) :])

        results = pl.pallas_call(
            body,
            grid_spec=pltpu.PrefetchScalarGridSpec(
                num_scalar_prefetch=len(self.scalars),
                grid=grid,
                in_specs=specs + [ANYWHERE] * len(waits) + [HELD] * len(keep),
                out_specs=list(out_specs or [HELD] * len(outs)),
                scratch_shapes=list(scratch),
            ),
            out_shape=list(outs),
            input_output_aliases={len(self.scalars) + i: o for i, o in aliases},
            compiler_params=pltpu.CompilerParams(vmem_limit_bytes=VMEM_MIB * 1024 * 1024),
            cost_estimate=pl.CostEstimate(
                flops=HEAVY if heavy else 1000, bytes_accessed=1000, transcendentals=0
            ),
        )(*self.scalars, *operands, *waits, *keep)
        self.last = results[0]
        return results

    def pass_on(self, value):
        def kernel(*refs):
            pass

        like = array(value.shape, value.dtype)
        return self(kernel, [value], [like], [ANYWHERE], [ANYWHERE], aliases=[(0, 0)])[0]


def load(order, *operands):
    parts = []
    for k, o in enumerate(operands):
        axis = max(range(o.ndim - 1), key=lambda i: o.shape[i])
        cuts = 4 if o.shape[axis] % 64 == 0 else 1
        size = o.shape[axis] // cuts
        for c in range(cuts):
            parts.append((k, (slice(None),) * axis + (pl.ds(c * size, size),)))

    def kernel(w, d, *refs):
        *refs, sems = refs
        n = len(operands)
        copies = [
            pltpu.make_async_copy(refs[k].at[at], refs[n + k].at[at], sems.at[i])
            for i, (k, at) in enumerate(parts)
        ]
        for copy in copies:
            copy.start()
        for copy in copies:
            copy.wait()

    return order(
        kernel,
        [pltpu.with_memory_space_constraint(o, pltpu.HBM) for o in operands],
        [held(o.shape, o.dtype) for o in operands],
        specs=[pl.BlockSpec(memory_space=pltpu.HBM)] * len(operands),
        scratch=[pltpu.SemaphoreType.DMA((len(parts),))],
        heavy=True,
    )


def encode(order, near, parts, readin, offset, cutoff):
    rows, width = parts[0].shape
    count = 2 * rows

    def kernel(w, d, own_ref, other_ref, readin_ref, offset_ref, cutoff_ref, act_ref, both):
        for ref, number in ((own_ref, w[CORE]), (other_ref, 1 - w[CORE])):
            both[span(number, rows), :] = ref[...]
        first = w[SIDE] if near else 1 - w[SIDE]
        pre = jnp.dot(both[...], readin_ref[0], preferred_element_type=F32)
        gate = cutoff_ref[0, span(first, count), :].astype(F32)
        act_ref[...] = ((pre + offset_ref[...]) * gate).astype(BF)

    return order(
        kernel,
        [*parts, readin, offset, cutoff],
        [held((count, readin.shape[-1]), BF)],
        scratch=[pltpu.VMEM((count, width), BF)],
        heavy=not near,
    )[0]


def turn(order, acts, parts):
    count, features = acts[0].shape
    rows, width = parts[0][0].shape

    def kernel(w, d, *refs):
        act_refs, part_refs, (turned_ref, tokens_ref) = refs[:2], refs[2:6], refs[6:]
        for half in range(2):
            turned_ref[:, half * count : (half + 1) * count] = act_refs[half][...].T
            for ref, number in zip(part_refs[2 * half : 2 * half + 2], (w[CORE], 1 - w[CORE])):
                tokens_ref[:, span(2 * half + number, rows)] = ref[...].T

    return order(
        kernel,
        [*acts, *parts[0], *parts[1]],
        [held((features, 2 * count), BF), held((width, 2 * count), BF)],
    )


def decode_near(order, away, act, writeout, hidden):
    count, features = act.shape
    blocks = 2
    rows = count // blocks
    dtype = BF if away else F32

    def kernel(w, d, act_ref, weight_ref, hidden_ref, *outs):
        target = 1 - w[CORE] if away else w[CORE]
        live = jnp.where(w[LAYER] <= d[target], 1.0, 0.0)
        out = jnp.dot(act_ref[...], weight_ref[0, target], preferred_element_type=F32)
        less = hidden_ref[target].astype(F32)
        owner = jnp.logical_and(w[LAYER] == 0, w[FEAT] == 0)
        for b, ref in enumerate(outs):
            mine = jnp.where(jnp.logical_and(owner, w[CORE] == b), 1.0, 0.0)
            ref[...] = ((out[b * rows : (b + 1) * rows] - mine * less) * live).astype(dtype)

    outs = [held((rows, writeout.shape[-1]), dtype)] * blocks
    return order(kernel, [act, writeout, hidden], outs)


def decode_far(order, away, other, act, writeout, cuts, heavy=False):
    count, features = act.shape
    rows = count // 2
    part = rows // cuts
    dtype = BF if away else F32

    def kernel(w, d, act_ref, weight_ref, *outs):
        target = 1 - w[CORE] if away else w[CORE]
        live = jnp.where(w[LAYER] <= d[target], 1.0, 0.0)
        block = act_ref[span(1 - w[FEAT] if other else w[FEAT], rows), :]
        out = jnp.dot(block, weight_ref[0, target], preferred_element_type=F32) * live
        for k, ref in enumerate(outs):
            ref[...] = out[k * part : (k + 1) * part].astype(dtype)

    outs = [held((part, writeout.shape[-1]), dtype)] * cuts
    return order(kernel, [act, writeout], outs, heavy=heavy)


def gradients(order, scaled, turned, writeout, lo, hi, sens=None, dec=None, last=None):
    targets, features, width = writeout.shape[1:]
    total, columns = scaled[0].shape
    count = total // 2
    block = block_of(features)
    at = lo // columns

    def kernel(w, d, *refs):
        refs = list(refs)
        s_refs = [refs.pop(0) for _ in range(targets)]
        turned_ref, weight_ref = refs.pop(0), refs.pop(0)
        sens_in = refs.pop(0) if sens is not None else None
        if last is not None:
            cutoff_ref, tokens_ref = refs.pop(0), refs.pop(0)
        if dec is not None:
            refs.pop(0)
        dec_ref = refs.pop(0)
        cols = span(pl.program_id(0), block)
        numbers = [w[CORE], 1 - w[CORE]]
        grad = 0.0 if sens_in is None else sens_in[:, cols]
        for ref, number in zip(s_refs, numbers):
            grad = grad + lax.dot_general(
                ref[...],
                weight_ref[0, number, cols, lo:hi],
                (((1,), (1,)), ((), ())),
                preferred_element_type=F32,
            )
        if last is None:
            refs[0][:, cols] = grad
        else:
            enc_ref, bias_ref, low_ref = refs
            biases = 0.0
            for half, side in enumerate((w[SIDE], 1 - w[SIDE])):
                rows = slice(half * count, (half + 1) * count)
                part = grad[rows] * cutoff_ref[0, span(side, count), cols].astype(F32)
                biases = biases + jnp.sum(part, axis=0, keepdims=True)
                low_ref[rows, :] = part.astype(BF)
            bias_ref[...] = biases
            enc_ref[0] = jnp.dot(
                tokens_ref[...], low_ref[...], preferred_element_type=F32
            ).astype(BF)
        for ref, number in zip(s_refs, numbers):
            out = jnp.dot(turned_ref[cols, :], ref[...], preferred_element_type=F32)
            dec_ref[0, number] = out.astype(BF)

    operands = [*scaled, turned, writeout]
    if sens is not None:
        operands.append(sens)
    if last is not None:
        operands += last
    specs = [HELD] * len(operands)
    aliases = []
    if dec is not None:
        aliases = [(len(operands), 0)]
        operands.append(dec)
        specs.append(ANYWHERE)
    out_specs = [pl.BlockSpec((1, targets, block, columns), lambda i, w, d: (0, 0, i, at))]
    outs = [array(writeout.shape, BF)]
    scratch = []
    if last is not None:
        out_specs.append(pl.BlockSpec((1, width, block), lambda i, w, d: (0, 0, i)))
        out_specs.append(pl.BlockSpec((1, block), lambda i, w, d: (0, i)))
        outs += [array((1, width, features), BF), array((1, features), F32)]
        scratch.append(pltpu.VMEM((total, block), BF))
    else:
        out_specs.append(HELD)
        outs.append(held((total, features), F32))
    results = order(
        kernel, operands, outs, specs, out_specs, (features // block,), scratch, aliases
    )
    if last is None:
        order.last = results[1]
    return results


def pick(flag, a, b):
    return jnp.where(flag, a, b)


def paired_shards(sizes, entries, readin, offset, cutoff, writeout, hidden, depth):
    layers, feats, toks = sizes
    layer, feat, tok = (lax.axis_index(a) for a in ("layer", "feat", "tok"))
    where = jnp.stack([tok // 2, tok % 2, feat, layer]).astype(jnp.int32)
    order = Order((where, depth))

    def to_core(a):
        return lax.ppermute(a, "tok", [(t, t ^ 1) for t in range(toks)])

    def to_side(a):
        return lax.ppermute(a, "tok", [(t, t ^ 2) for t in range(toks)])

    def mixed(first):
        pairs = []
        for f in range(feats):
            for t in range(toks):
                over_side = (t % 2 == 0) == first
                goal = (f, t ^ 2) if over_side else (f ^ 1, t)
                pairs.append((f * toks + t, goal[0] * toks + goal[1]))
        return lambda a: lax.ppermute(a, ("feat", "tok"), pairs)

    to_first, to_second = mixed(True), mixed(False)
    binary = layers & (layers - 1) == 0

    def layer_goal(l, s):
        return l ^ s if binary else lax.rem(l + s, layers)

    def layer_source(l, s):
        return l ^ s if binary else lax.rem(l - s + layers, layers)

    def to_layer(a, s):
        return lax.ppermute(
            a, "layer", [(l, l ^ s if binary else (l + s) % layers) for l in range(layers)]
        )

    own = entries[0]
    rows, width = own.shape
    total = rows * toks
    inverse = 1.0 / math.sqrt(total)
    piece = rows // layers
    chunks = column_chunks(width)

    far = to_side(own)
    near = to_core(own)
    readin, cutoff, writeout, hidden = load(order, readin, cutoff, writeout, hidden)
    act_near = encode(order, True, (own, near), readin, offset, cutoff)

    away = decode_near(order, True, act_near, writeout, hidden)
    here_got = [to_core(a) for a in away]
    here = [*decode_near(order, False, act_near, writeout, hidden), *here_got]
    far = order.pass_on(far)

    def first_kernel(w, d, kept0, kept1, got0, got1, *outs):
        y1 = w[FEAT] == 1
        other = pick(y1, kept0[...], kept1[...]) + pick(y1, got0[...], got1[...]).astype(F32)
        for (lo, hi), out in zip(chunks, outs):
            out[...] = other[:, lo:hi].astype(BF)

    sends = order(first_kernel, here, [held((rows, hi - lo), BF) for lo, hi in chunks])
    got_first = [to_first(send) for send in sends]

    far_near = to_core(far)
    act_far = encode(order, False, (far, far_near), readin, offset, cutoff)

    def far_block(other, cuts):
        away = decode_far(order, True, other, act_far, writeout, cuts)
        got = [to_core(a) for a in away]
        return (*decode_far(order, False, other, act_far, writeout, 1), *got)

    def joined_rows(refs, at):
        return jnp.concatenate([ref[:, at] for ref in refs]).astype(F32)

    there_other = far_block(True, 2)

    def reduce_sides(lo, hi, got_first, heavy):
        size = hi - lo
        at = slice(lo, hi)

        def second_kernel(w, d, hk0, hk1, hg0, hg1, first, tk, *refs):
            *tg, out_first, out_second = refs
            y0 = w[FEAT] == 0
            here_y = pick(y0, hk0[:, at], hk1[:, at])
            here_y += pick(y0, hg0[:, at], hg1[:, at]).astype(F32)
            there_other = tk[:, at] + joined_rows(tg, at)
            zero = w[CORE] == 0
            out_first[...] = pick(zero, here_y, there_other).astype(BF)
            rest = pick(zero, there_other, here_y) + first[...].astype(F32)
            out_second[...] = rest.astype(BF)

        operands = (*here, got_first, *there_other)
        sends = order(second_kernel, operands, [held((rows, size), BF)] * 2, heavy=heavy)
        return lo, hi, to_first(sends[0]), to_second(sends[1])

    def send_pieces(lo, hi, got, got_second, heavy):
        size = hi - lo

        def kernel(w, d, *refs):
            tk, *tg = refs[: len(there)]
            first, second, mine, *outs, kept = refs[len(there) :]
            kept[...] = (
                tk[:, lo:hi]
                + joined_rows(tg, slice(lo, hi))
                + first[...].astype(F32)
                + second[...].astype(F32)
            )
            mine[...] = kept[span(w[LAYER], piece), :]
            for s, out in enumerate(outs, 1):
                out[...] = kept[span(layer_goal(w[LAYER], s), piece), :].astype(BF)

        outs = [held((piece, size), F32)] + [held((piece, size), BF)] * (layers - 1)
        scratch = [pltpu.VMEM((rows, size), F32)]
        mine, *outs = order(
            kernel, (*there, got, got_second), outs, scratch=scratch, heavy=heavy
        )
        return mine, [to_layer(out, s) for s, out in enumerate(outs, 1)]

    def scale_piece(mine, pieces):
        def kernel(w, d, mine_ref, *refs):
            *refs, out = refs
            value = mine_ref[...]
            for ref in refs:
                value = value + ref[...].astype(F32)
            out[...] = (value * inverse).astype(BF)

        scaled = order(kernel, (mine, *pieces), [held(mine.shape, BF)], heavy=True)[0]
        return scaled, [to_layer(scaled, s) for s in range(1, layers)]

    def join_pieces(scaled, pieces):
        size = scaled.shape[1]

        def kernel(w, d, *refs):
            *refs, out = refs
            out[span(w[LAYER], piece), :] = refs[0][...]
            for s, ref in enumerate(refs[1:], 1):
                out[span(layer_source(w[LAYER], s), piece), :] = ref[...]

        done = order(kernel, (scaled, *pieces), [held((rows, size), BF)], heavy=True)[0]
        return done, to_second(done)

    def join_pair(done, got):
        def kernel(w, d, done_ref, got_ref, out0, out1):
            done_last = jnp.logical_or(w[CORE] == 1, w[FEAT] == 1)
            out0[...] = pick(done_last, got_ref[...], done_ref[...])
            out1[...] = pick(done_last, done_ref[...], got_ref[...])

        pair = order(kernel, (done, got), [held(done.shape, BF)] * 2, heavy=True)
        return pair, [to_first(block) for block in pair]

    def join_all(pair, got):
        def kernel(w, d, pair0, pair1, got0, got1, out):
            zero = w[CORE] == 0
            y = w[FEAT]
            live = jnp.where(w[LAYER] <= d[w[CORE]], 1.0, 0.0).astype(BF)
            for ref, number in (
                (pair0, pick(zero, 2, y)),
                (pair1, pick(zero, 3, 2 + y)),
                (got0, pick(zero, 0, 1 - y)),
                (got1, pick(zero, 1, 3 - y)),
            ):
                out[span(number, rows), :] = ref[...] * live

        size = pair[0].shape[1]
        full = order(kernel, (*pair, *got), [held((total, size), BF)], heavy=True)[0]
        return full, to_core(full)

    reduced = [
        reduce_sides(*chunk, got, k > 0) for k, (chunk, got) in enumerate(zip(chunks, got_first))
    ]
    there = far_block(False, 4)
    turned, tokens = turn(order, (act_near, act_far), ((own, near), (far, far_near)))
    order.keep = [writeout, cutoff, turned, tokens]
    stages = [send_pieces(*r, k > 0) for k, r in enumerate(reduced)]
    stages = [scale_piece(*stage) for stage in stages]
    stages = [join_pieces(*stage) for stage in stages]
    stages = [join_pair(*stage) for stage in stages]
    scaled = [join_all(*stage) for stage in stages]
    order.keep = []
    sens = dec = None
    for k, (lo, hi) in enumerate(chunks):
        last = (cutoff, tokens) if k == len(chunks) - 1 else None
        dec, *rest = gradients(order, scaled[k], turned, writeout, lo, hi, sens, dec, last)
        sens = rest[0]
    return rest[0], dec, rest[1]


def solution(mesh):
    sizes = tuple(mesh.shape[a] for a in ("layer", "feat", "tok"))

    def shards(*args):
        rows = args[0].shape[1]
        targets = args[4].shape[1]
        paired = sizes[1] == targets == 2 and sizes[2] == 4
        if paired and rows % ROWS_UNIT == 0 and rows % (16 * sizes[0]) == 0:
            return paired_shards(sizes, *args)
        return plain_shards(*args)

    return jax.shard_map(
        shards,
        mesh=mesh,
        in_specs=(
            P("layer", "tok", None),
            P("layer", None, ("feat", "tok")),
            P("layer", ("feat", "tok")),
            P("layer", None, ("feat", "tok")),
            P("layer", None, ("feat", "tok"), None),
            P(None, "tok", None),
            P(),
        ),
        out_specs=(
            P("layer", None, ("feat", "tok")),
            P("layer", None, ("feat", "tok"), None),
            P("layer", ("feat", "tok")),
        ),
        check_vma=False,
    )
```

```python
import math

import jax
import jax.numpy as jnp
from jax import lax
from jax.experimental import pallas as pl
from jax.experimental.pallas import tpu as pltpu
from jax.sharding import PartitionSpec as P

BF = jnp.bfloat16
F32 = jnp.float32


def plain_shards(entries, readin, offset, cutoff, writeout, hidden, depth):
    layer = lax.axis_index("layer")
    owner = jnp.logical_and(layer == 0, lax.axis_index("feat") == 0).astype(F32)
    gathered = lax.all_gather(entries, "tok", axis=1, tiled=True)[0]
    inverse = 1.0 / math.sqrt(gathered.shape[0])
    gate = cutoff[0].astype(F32)
    pre = jnp.dot(gathered, readin[0], preferred_element_type=F32) + offset[0][None, :]
    act = (pre * gate).astype(BF)
    live = (layer <= depth).astype(F32)
    targets = writeout.shape[1]
    partials = jnp.stack(
        [jnp.dot(act, writeout[0, t], preferred_element_type=F32) for t in range(targets)]
    )
    rows = hidden.shape[1]
    start = lax.axis_index("tok") * rows
    current = lax.dynamic_slice_in_dim(partials, start, rows, 1)
    partials = lax.dynamic_update_slice_in_dim(
        partials, current - owner * hidden.astype(F32), start, 1
    )
    summed = lax.psum_scatter(
        partials * live[:, None, None], ("feat", "tok"), scatter_dimension=1, tiled=True
    )
    summed = lax.psum(summed, "layer")
    scaled = lax.all_gather((summed * inverse).astype(BF), ("feat", "tok"), axis=1, tiled=True)
    dec = [
        (jnp.einsum("tf,td->fd", act, scaled[t], preferred_element_type=F32) * live[t]).astype(BF)
        for t in range(targets)
    ]
    sens = sum(
        live[t] * jnp.einsum("td,fd->tf", scaled[t], writeout[0, t], preferred_element_type=F32)
        for t in range(targets)
    )
    pre_grad = sens * gate
    enc = jnp.einsum("td,tf->df", gathered, pre_grad.astype(BF), preferred_element_type=F32)
    return enc.astype(BF)[None], jnp.stack(dec)[None], jnp.sum(pre_grad, axis=0)[None]


def column_chunks(width):
    for parts in (3, 2):
        if width % (128 * parts) == 0:
            unit = width // parts
            return [(0, width - unit), (width - unit, width)]
    return [(0, width)]


VMEM_MIB = 16
FEATURE_BLOCK = 512
ROWS_UNIT = 128
HEAVY = 10**11
SIDE, CORE, FEAT, LAYER = range(4)
HELD = pl.BlockSpec(memory_space=pltpu.VMEM)
ANYWHERE = pl.BlockSpec(memory_space=pl.ANY)


def held(shape, dtype):
    return pltpu.VMEM(shape, dtype)


def array(shape, dtype):
    return jax.ShapeDtypeStruct(shape, dtype)


def block_of(features):
    return FEATURE_BLOCK if features % FEATURE_BLOCK == 0 else features


def span(number, size):
    return pl.ds(pl.multiple_of(number * size, size), size)


class Order:
    def __init__(self, scalars):
        self.scalars = scalars
        self.last = None
        self.keep = []

    def __call__(
        self,
        kernel,
        operands,
        outs,
        specs=None,
        out_specs=None,
        grid=(1,),
        scratch=(),
        aliases=(),
        heavy=False,
    ):
        count = len(operands)
        operands = list(operands)
        specs = list(specs or [HELD] * count)
        waits = [] if self.last is None else [self.last]
        keep = [k for k in self.keep if all(k is not o for o in operands)]

        def body(*refs):
            at = len(self.scalars) + count
            kernel(*refs[:at], *refs[at + len(waits) + len(keep) :])

        results = pl.pallas_call(
            body,
            grid_spec=pltpu.PrefetchScalarGridSpec(
                num_scalar_prefetch=len(self.scalars),
                grid=grid,
                in_specs=specs + [ANYWHERE] * len(waits) + [HELD] * len(keep),
                out_specs=list(out_specs or [HELD] * len(outs)),
                scratch_shapes=list(scratch),
            ),
            out_shape=list(outs),
            input_output_aliases={len(self.scalars) + i: o for i, o in aliases},
            compiler_params=pltpu.CompilerParams(vmem_limit_bytes=VMEM_MIB * 1024 * 1024),
            cost_estimate=pl.CostEstimate(
                flops=HEAVY if heavy else 1000, bytes_accessed=1000, transcendentals=0
            ),
        )(*self.scalars, *operands, *waits, *keep)
        self.last = results[0]
        return results

    def pass_on(self, value):
        def kernel(*refs):
            pass

        like = array(value.shape, value.dtype)
        return self(kernel, [value], [like], [ANYWHERE], [ANYWHERE], aliases=[(0, 0)])[0]


def load(order, *operands):
    parts = []
    for k, o in enumerate(operands):
        axis = max(range(o.ndim - 1), key=lambda i: o.shape[i])
        cuts = 4 if o.shape[axis] % 64 == 0 else 1
        size = o.shape[axis] // cuts
        for c in range(cuts):
            parts.append((k, (slice(None),) * axis + (pl.ds(c * size, size),)))

    def kernel(w, d, *refs):
        *refs, sems = refs
        n = len(operands)
        copies = [
            pltpu.make_async_copy(refs[k].at[at], refs[n + k].at[at], sems.at[i])
            for i, (k, at) in enumerate(parts)
        ]
        for copy in copies:
            copy.start()
        for copy in copies:
            copy.wait()

    return order(
        kernel,
        [pltpu.with_memory_space_constraint(o, pltpu.HBM) for o in operands],
        [held(o.shape, o.dtype) for o in operands],
        specs=[pl.BlockSpec(memory_space=pltpu.HBM)] * len(operands),
        scratch=[pltpu.SemaphoreType.DMA((len(parts),))],
        heavy=True,
    )


def encode(order, near, parts, readin, offset, cutoff):
    rows, width = parts[0].shape
    count = 2 * rows

    def kernel(w, d, own_ref, other_ref, readin_ref, offset_ref, cutoff_ref, act_ref, both):
        for ref, number in ((own_ref, w[CORE]), (other_ref, 1 - w[CORE])):
            both[span(number, rows), :] = ref[...]
        first = w[SIDE] if near else 1 - w[SIDE]
        pre = jnp.dot(both[...], readin_ref[0], preferred_element_type=F32)
        gate = cutoff_ref[0, span(first, count), :].astype(F32)
        act_ref[...] = ((pre + offset_ref[...]) * gate).astype(BF)

    return order(
        kernel,
        [*parts, readin, offset, cutoff],
        [held((count, readin.shape[-1]), BF)],
        scratch=[pltpu.VMEM((count, width), BF)],
        heavy=not near,
    )[0]


def turn(order, acts, parts):
    count, features = acts[0].shape
    rows, width = parts[0][0].shape

    def kernel(w, d, *refs):
        act_refs, part_refs, (turned_ref, tokens_ref) = refs[:2], refs[2:6], refs[6:]
        for half in range(2):
            turned_ref[:, half * count : (half + 1) * count] = act_refs[half][...].T
            for ref, number in zip(part_refs[2 * half : 2 * half + 2], (w[CORE], 1 - w[CORE])):
                tokens_ref[:, span(2 * half + number, rows)] = ref[...].T

    return order(
        kernel,
        [*acts, *parts[0], *parts[1]],
        [held((features, 2 * count), BF), held((width, 2 * count), BF)],
    )


def decode_near(order, away, act, writeout, hidden):
    count, features = act.shape
    blocks = 2
    rows = count // blocks
    dtype = BF if away else F32

    def kernel(w, d, act_ref, weight_ref, hidden_ref, *outs):
        target = 1 - w[CORE] if away else w[CORE]
        live = jnp.where(w[LAYER] <= d[target], 1.0, 0.0)
        out = jnp.dot(act_ref[...], weight_ref[0, target], preferred_element_type=F32)
        less = hidden_ref[target].astype(F32)
        owner = jnp.logical_and(w[LAYER] == 0, w[FEAT] == 0)
        for b, ref in enumerate(outs):
            mine = jnp.where(jnp.logical_and(owner, w[CORE] == b), 1.0, 0.0)
            ref[...] = ((out[b * rows : (b + 1) * rows] - mine * less) * live).astype(dtype)

    outs = [held((rows, writeout.shape[-1]), dtype)] * blocks
    return order(kernel, [act, writeout, hidden], outs)


def decode_far(order, away, other, act, writeout, cuts, heavy=False):
    count, features = act.shape
    rows = count // 2
    part = rows // cuts
    dtype = BF if away else F32

    def kernel(w, d, act_ref, weight_ref, *outs):
        target = 1 - w[CORE] if away else w[CORE]
        live = jnp.where(w[LAYER] <= d[target], 1.0, 0.0)
        block = act_ref[span(1 - w[FEAT] if other else w[FEAT], rows), :]
        out = jnp.dot(block, weight_ref[0, target], preferred_element_type=F32) * live
        for k, ref in enumerate(outs):
            ref[...] = out[k * part : (k + 1) * part].astype(dtype)

    outs = [held((part, writeout.shape[-1]), dtype)] * cuts
    return order(kernel, [act, writeout], outs, heavy=heavy)


def target_gradients(order, mine, scaled, turned, writeout, lo, hi, sens, dec):
    features = writeout.shape[2]
    total, columns = scaled.shape
    block = block_of(features)
    at = lo // columns

    def target(w):
        return w[CORE] if mine else 1 - w[CORE]

    def kernel(w, d, s_ref, turned_ref, weight_ref, *refs):
        dec_ref, out_ref = refs[-2:]
        cols = span(pl.program_id(0), block)
        grad = lax.dot_general(
            s_ref[...],
            weight_ref[0, target(w), cols, lo:hi],
            (((1,), (1,)), ((), ())),
            preferred_element_type=F32,
        )
        out_ref[:, cols] = grad if sens is None else refs[0][:, cols] + grad
        out = jnp.dot(turned_ref[cols, :], s_ref[...], preferred_element_type=F32)
        dec_ref[0, 0] = out.astype(BF)

    operands = [scaled, turned, writeout] + ([] if sens is None else [sens])
    before = [] if dec is None else [dec]
    dec, sens = order(
        kernel,
        operands + before,
        [array(writeout.shape, BF), held((total, features), F32)],
        [HELD] * len(operands) + [ANYWHERE] * len(before),
        [pl.BlockSpec((1, 1, block, columns), lambda i, w, d: (0, target(w), i, at)), HELD],
        grid=(features // block,),
        aliases=[(len(operands), 0)] if before else (),
    )
    order.last = sens
    return dec, sens


def gradients(order, scaled, turned, writeout, lo, hi, sens=None, dec=None, last=None):
    targets, features, width = writeout.shape[1:]
    total, columns = scaled[0].shape
    count = total // 2
    block = block_of(features)
    at = lo // columns

    def kernel(w, d, *refs):
        refs = list(refs)
        s_refs = [refs.pop(0) for _ in range(targets)]
        turned_ref, weight_ref = refs.pop(0), refs.pop(0)
        sens_in = refs.pop(0) if sens is not None else None
        if last is not None:
            cutoff_ref, tokens_ref = refs.pop(0), refs.pop(0)
        if dec is not None:
            refs.pop(0)
        dec_ref = refs.pop(0)
        cols = span(pl.program_id(0), block)
        numbers = [w[CORE], 1 - w[CORE]]
        grad = 0.0 if sens_in is None else sens_in[:, cols]
        for ref, number in zip(s_refs, numbers):
            grad = grad + lax.dot_general(
                ref[...],
                weight_ref[0, number, cols, lo:hi],
                (((1,), (1,)), ((), ())),
                preferred_element_type=F32,
            )
        if last is None:
            refs[0][:, cols] = grad
        else:
            enc_ref, bias_ref, low_ref = refs
            biases = 0.0
            for half, side in enumerate((w[SIDE], 1 - w[SIDE])):
                rows = slice(half * count, (half + 1) * count)
                part = grad[rows] * cutoff_ref[0, span(side, count), cols].astype(F32)
                biases = biases + jnp.sum(part, axis=0, keepdims=True)
                low_ref[rows, :] = part.astype(BF)
            bias_ref[...] = biases
            enc_ref[0] = jnp.dot(
                tokens_ref[...], low_ref[...], preferred_element_type=F32
            ).astype(BF)
        for ref, number in zip(s_refs, numbers):
            out = jnp.dot(turned_ref[cols, :], ref[...], preferred_element_type=F32)
            dec_ref[0, number] = out.astype(BF)

    operands = [*scaled, turned, writeout]
    if sens is not None:
        operands.append(sens)
    if last is not None:
        operands += last
    specs = [HELD] * len(operands)
    aliases = []
    if dec is not None:
        aliases = [(len(operands), 0)]
        operands.append(dec)
        specs.append(ANYWHERE)
    out_specs = [pl.BlockSpec((1, targets, block, columns), lambda i, w, d: (0, 0, i, at))]
    outs = [array(writeout.shape, BF)]
    scratch = []
    if last is not None:
        out_specs.append(pl.BlockSpec((1, width, block), lambda i, w, d: (0, 0, i)))
        out_specs.append(pl.BlockSpec((1, block), lambda i, w, d: (0, i)))
        outs += [array((1, width, features), BF), array((1, features), F32)]
        scratch.append(pltpu.VMEM((total, block), BF))
    else:
        out_specs.append(HELD)
        outs.append(held((total, features), F32))
    results = order(
        kernel, operands, outs, specs, out_specs, (features // block,), scratch, aliases
    )
    if last is None:
        order.last = results[1]
    return results


def pick(flag, a, b):
    return jnp.where(flag, a, b)


def paired_shards(sizes, entries, readin, offset, cutoff, writeout, hidden, depth):
    layers, feats, toks = sizes
    layer, feat, tok = (lax.axis_index(a) for a in ("layer", "feat", "tok"))
    where = jnp.stack([tok // 2, tok % 2, feat, layer]).astype(jnp.int32)
    order = Order((where, depth))

    def to_core(a):
        return lax.ppermute(a, "tok", [(t, t ^ 1) for t in range(toks)])

    def to_side(a):
        return lax.ppermute(a, "tok", [(t, t ^ 2) for t in range(toks)])

    def mixed(first):
        pairs = []
        for f in range(feats):
            for t in range(toks):
                over_side = (t % 2 == 0) == first
                goal = (f, t ^ 2) if over_side else (f ^ 1, t)
                pairs.append((f * toks + t, goal[0] * toks + goal[1]))
        return lambda a: lax.ppermute(a, ("feat", "tok"), pairs)

    to_first, to_second = mixed(True), mixed(False)
    binary = layers & (layers - 1) == 0

    def layer_goal(l, s):
        return l ^ s if binary else lax.rem(l + s, layers)

    def layer_source(l, s):
        return l ^ s if binary else lax.rem(l - s + layers, layers)

    def to_layer(a, s):
        return lax.ppermute(
            a, "layer", [(l, l ^ s if binary else (l + s) % layers) for l in range(layers)]
        )

    own = entries[0]
    rows, width = own.shape
    total = rows * toks
    inverse = 1.0 / math.sqrt(total)
    piece = rows // layers
    chunks = column_chunks(width)

    far = to_side(own)
    near = to_core(own)
    readin, cutoff, writeout, hidden = load(order, readin, cutoff, writeout, hidden)
    act_near = encode(order, True, (own, near), readin, offset, cutoff)

    away = decode_near(order, True, act_near, writeout, hidden)
    here_got = [to_core(a) for a in away]
    here = [*decode_near(order, False, act_near, writeout, hidden), *here_got]
    far = order.pass_on(far)

    def first_kernel(w, d, kept0, kept1, got0, got1, *outs):
        y1 = w[FEAT] == 1
        other = pick(y1, kept0[...], kept1[...]) + pick(y1, got0[...], got1[...]).astype(F32)
        for (lo, hi), out in zip(chunks, outs):
            out[...] = other[:, lo:hi].astype(BF)

    sends = order(first_kernel, here, [held((rows, hi - lo), BF) for lo, hi in chunks])
    got_first = [to_first(send) for send in sends]

    far_near = to_core(far)
    act_far = encode(order, False, (far, far_near), readin, offset, cutoff)

    def far_block(other, cuts):
        away = decode_far(order, True, other, act_far, writeout, cuts)
        got = [to_core(a) for a in away]
        return (*decode_far(order, False, other, act_far, writeout, 1), *got)

    def joined_rows(refs, at):
        return jnp.concatenate([ref[:, at] for ref in refs]).astype(F32)

    there_other = far_block(True, 2)

    def reduce_sides(lo, hi, got_first, heavy):
        size = hi - lo
        at = slice(lo, hi)

        def second_kernel(w, d, hk0, hk1, hg0, hg1, first, tk, *refs):
            *tg, out_first, out_second = refs
            y0 = w[FEAT] == 0
            here_y = pick(y0, hk0[:, at], hk1[:, at])
            here_y += pick(y0, hg0[:, at], hg1[:, at]).astype(F32)
            there_other = tk[:, at] + joined_rows(tg, at)
            zero = w[CORE] == 0
            out_first[...] = pick(zero, here_y, there_other).astype(BF)
            rest = pick(zero, there_other, here_y) + first[...].astype(F32)
            out_second[...] = rest.astype(BF)

        operands = (*here, got_first, *there_other)
        sends = order(second_kernel, operands, [held((rows, size), BF)] * 2, heavy=heavy)
        return lo, hi, to_first(sends[0]), to_second(sends[1])

    def send_pieces(lo, hi, got, got_second, heavy):
        size = hi - lo

        def kernel(w, d, *refs):
            tk, *tg = refs[: len(there)]
            first, second, mine, *outs, kept = refs[len(there) :]
            kept[...] = (
                tk[:, lo:hi]
                + joined_rows(tg, slice(lo, hi))
                + first[...].astype(F32)
                + second[...].astype(F32)
            )
            mine[...] = kept[span(w[LAYER], piece), :]
            for s, out in enumerate(outs, 1):
                out[...] = kept[span(layer_goal(w[LAYER], s), piece), :].astype(BF)

        outs = [held((piece, size), F32)] + [held((piece, size), BF)] * (layers - 1)
        scratch = [pltpu.VMEM((rows, size), F32)]
        mine, *outs = order(
            kernel, (*there, got, got_second), outs, scratch=scratch, heavy=heavy
        )
        return mine, [to_layer(out, s) for s, out in enumerate(outs, 1)]

    def scale_piece(mine, pieces):
        def kernel(w, d, mine_ref, *refs):
            *refs, out = refs
            value = mine_ref[...]
            for ref in refs:
                value = value + ref[...].astype(F32)
            out[...] = (value * inverse).astype(BF)

        scaled = order(kernel, (mine, *pieces), [held(mine.shape, BF)], heavy=True)[0]
        return scaled, [to_layer(scaled, s) for s in range(1, layers)]

    def join_pieces(scaled, pieces):
        size = scaled.shape[1]

        def kernel(w, d, *refs):
            *refs, out = refs
            out[span(w[LAYER], piece), :] = refs[0][...]
            for s, ref in enumerate(refs[1:], 1):
                out[span(layer_source(w[LAYER], s), piece), :] = ref[...]

        done = order(kernel, (scaled, *pieces), [held((rows, size), BF)], heavy=True)[0]
        return done, to_second(done)

    def join_pair(done, got, heavy):
        def kernel(w, d, done_ref, got_ref, out0, out1):
            done_last = jnp.logical_or(w[CORE] == 1, w[FEAT] == 1)
            out0[...] = pick(done_last, got_ref[...], done_ref[...])
            out1[...] = pick(done_last, done_ref[...], got_ref[...])

        pair = order(kernel, (done, got), [held(done.shape, BF)] * 2, heavy=heavy)
        return pair, [to_first(block) for block in pair]

    def join_all(pair, got):
        def kernel(w, d, pair0, pair1, got0, got1, out):
            zero = w[CORE] == 0
            y = w[FEAT]
            live = jnp.where(w[LAYER] <= d[w[CORE]], 1.0, 0.0).astype(BF)
            for ref, number in (
                (pair0, pick(zero, 2, y)),
                (pair1, pick(zero, 3, 2 + y)),
                (got0, pick(zero, 0, 1 - y)),
                (got1, pick(zero, 1, 3 - y)),
            ):
                out[span(number, rows), :] = ref[...] * live

        size = pair[0].shape[1]
        full = order(kernel, (*pair, *got), [held((total, size), BF)], heavy=True)[0]
        return full, to_core(full)

    reduced = [
        reduce_sides(*chunk, got, k > 0) for k, (chunk, got) in enumerate(zip(chunks, got_first))
    ]
    there = far_block(False, 4)
    turned, tokens = turn(order, (act_near, act_far), ((own, near), (far, far_near)))
    order.keep = [writeout, cutoff, turned, tokens]
    count = len(chunks)
    sent, joined, pairs = send_pieces(*reduced[0], False), [], []
    for k in range(count):
        scaled = scale_piece(*sent)
        if k + 1 < count:
            sent = send_pieces(*reduced[k + 1], True)
        if k > 0:
            pairs.append(join_pair(*joined[k - 1], True))
        joined.append(join_pieces(*scaled))
    pairs.append(join_pair(*joined[-1], False))
    scaled = join_all(*pairs[0])
    sens = dec = None
    for k, (lo, hi) in enumerate(chunks[:-1]):
        own, other = scaled
        dec, sens = target_gradients(order, True, own, turned, writeout, lo, hi, sens, dec)
        following = join_all(*pairs[k + 1])
        dec, sens = target_gradients(order, False, other, turned, writeout, lo, hi, sens, dec)
        scaled = following
    order.keep = []
    lo, hi = chunks[-1]
    dec, enc, bias = gradients(
        order, scaled, turned, writeout, lo, hi, sens, dec, (cutoff, tokens)
    )
    return enc, dec, bias


def solution(mesh):
    sizes = tuple(mesh.shape[a] for a in ("layer", "feat", "tok"))

    def shards(*args):
        rows = args[0].shape[1]
        targets = args[4].shape[1]
        paired = sizes[1] == targets == 2 and sizes[2] == 4
        if paired and rows % ROWS_UNIT == 0 and rows % (16 * sizes[0]) == 0:
            return paired_shards(sizes, *args)
        return plain_shards(*args)

    return jax.shard_map(
        shards,
        mesh=mesh,
        in_specs=(
            P("layer", "tok", None),
            P("layer", None, ("feat", "tok")),
            P("layer", ("feat", "tok")),
            P("layer", None, ("feat", "tok")),
            P("layer", None, ("feat", "tok"), None),
            P(None, "tok", None),
            P(),
        ),
        out_specs=(
            P("layer", None, ("feat", "tok")),
            P("layer", None, ("feat", "tok"), None),
            P("layer", ("feat", "tok")),
        ),
        check_vma=False,
    )
```

```python
import math

import jax
import jax.numpy as jnp
from jax import lax
from jax.experimental import pallas as pl
from jax.experimental.pallas import tpu as pltpu
from jax.sharding import PartitionSpec as P

BF = jnp.bfloat16
F32 = jnp.float32


def plain_shards(entries, readin, offset, cutoff, writeout, hidden, depth):
    layer = lax.axis_index("layer")
    owner = jnp.logical_and(layer == 0, lax.axis_index("feat") == 0).astype(F32)
    gathered = lax.all_gather(entries, "tok", axis=1, tiled=True)[0]
    inverse = 1.0 / math.sqrt(gathered.shape[0])
    gate = cutoff[0].astype(F32)
    pre = jnp.dot(gathered, readin[0], preferred_element_type=F32) + offset[0][None, :]
    act = (pre * gate).astype(BF)
    live = (layer <= depth).astype(F32)
    targets = writeout.shape[1]
    partials = jnp.stack(
        [jnp.dot(act, writeout[0, t], preferred_element_type=F32) for t in range(targets)]
    )
    rows = hidden.shape[1]
    start = lax.axis_index("tok") * rows
    current = lax.dynamic_slice_in_dim(partials, start, rows, 1)
    partials = lax.dynamic_update_slice_in_dim(
        partials, current - owner * hidden.astype(F32), start, 1
    )
    summed = lax.psum_scatter(
        partials * live[:, None, None], ("feat", "tok"), scatter_dimension=1, tiled=True
    )
    summed = lax.psum(summed, "layer")
    scaled = lax.all_gather((summed * inverse).astype(BF), ("feat", "tok"), axis=1, tiled=True)
    dec = [
        (jnp.einsum("tf,td->fd", act, scaled[t], preferred_element_type=F32) * live[t]).astype(BF)
        for t in range(targets)
    ]
    sens = sum(
        live[t] * jnp.einsum("td,fd->tf", scaled[t], writeout[0, t], preferred_element_type=F32)
        for t in range(targets)
    )
    pre_grad = sens * gate
    enc = jnp.einsum("td,tf->df", gathered, pre_grad.astype(BF), preferred_element_type=F32)
    return enc.astype(BF)[None], jnp.stack(dec)[None], jnp.sum(pre_grad, axis=0)[None]


def column_chunks(width):
    for parts in (3, 2):
        if width % (128 * parts) == 0:
            unit = width // parts
            return [(0, width - unit), (width - unit, width)]
    return [(0, width)]


VMEM_MIB = 16
FEATURE_BLOCK = 512
ROWS_UNIT = 128
HEAVY = 10**11
SIDE, CORE, FEAT, LAYER = range(4)
HELD = pl.BlockSpec(memory_space=pltpu.VMEM)
ANYWHERE = pl.BlockSpec(memory_space=pl.ANY)


def held(shape, dtype):
    return pltpu.VMEM(shape, dtype)


def array(shape, dtype):
    return jax.ShapeDtypeStruct(shape, dtype)


def block_of(features):
    return FEATURE_BLOCK if features % FEATURE_BLOCK == 0 else features


def span(number, size):
    return pl.ds(pl.multiple_of(number * size, size), size)


class Order:
    def __init__(self, scalars):
        self.scalars = scalars
        self.last = None
        self.keep = []

    def __call__(
        self,
        kernel,
        operands,
        outs,
        specs=None,
        out_specs=None,
        grid=(1,),
        scratch=(),
        aliases=(),
        heavy=False,
        wait=(),
    ):
        count = len(operands)
        operands = list(operands)
        specs = list(specs or [HELD] * count)
        waits = [*([] if self.last is None else [self.last]), *wait]
        keep = [k for k in self.keep if all(k is not o for o in operands)]

        def body(*refs):
            at = len(self.scalars) + count
            kernel(*refs[:at], *refs[at + len(waits) + len(keep) :])

        results = pl.pallas_call(
            body,
            grid_spec=pltpu.PrefetchScalarGridSpec(
                num_scalar_prefetch=len(self.scalars),
                grid=grid,
                in_specs=specs + [ANYWHERE] * len(waits) + [HELD] * len(keep),
                out_specs=list(out_specs or [HELD] * len(outs)),
                scratch_shapes=list(scratch),
            ),
            out_shape=list(outs),
            input_output_aliases={len(self.scalars) + i: o for i, o in aliases},
            compiler_params=pltpu.CompilerParams(vmem_limit_bytes=VMEM_MIB * 1024 * 1024),
            cost_estimate=pl.CostEstimate(
                flops=HEAVY if heavy else 1000, bytes_accessed=1000, transcendentals=0
            ),
        )(*self.scalars, *operands, *waits, *keep)
        self.last = results[0]
        return results

    def pass_on(self, value):
        def kernel(*refs):
            pass

        like = array(value.shape, value.dtype)
        return self(kernel, [value], [like], [ANYWHERE], [ANYWHERE], aliases=[(0, 0)])[0]


def load(order, *operands):
    parts = []
    for k, o in enumerate(operands):
        axis = max(range(o.ndim - 1), key=lambda i: o.shape[i])
        cuts = 4 if o.shape[axis] % 64 == 0 else 1
        size = o.shape[axis] // cuts
        for c in range(cuts):
            parts.append((k, (slice(None),) * axis + (pl.ds(c * size, size),)))

    def kernel(w, d, *refs):
        *refs, sems = refs
        n = len(operands)
        copies = [
            pltpu.make_async_copy(refs[k].at[at], refs[n + k].at[at], sems.at[i])
            for i, (k, at) in enumerate(parts)
        ]
        for copy in copies:
            copy.start()
        for copy in copies:
            copy.wait()

    return order(
        kernel,
        [pltpu.with_memory_space_constraint(o, pltpu.HBM) for o in operands],
        [held(o.shape, o.dtype) for o in operands],
        specs=[pl.BlockSpec(memory_space=pltpu.HBM)] * len(operands),
        scratch=[pltpu.SemaphoreType.DMA((len(parts),))],
        heavy=True,
    )


def encode(order, near, parts, readin, offset, cutoff):
    rows, width = parts[0].shape
    count = 2 * rows

    def kernel(w, d, own_ref, other_ref, readin_ref, offset_ref, cutoff_ref, act_ref, both):
        for ref, number in ((own_ref, w[CORE]), (other_ref, 1 - w[CORE])):
            both[span(number, rows), :] = ref[...]
        first = w[SIDE] if near else 1 - w[SIDE]
        pre = jnp.dot(both[...], readin_ref[0], preferred_element_type=F32)
        gate = cutoff_ref[0, span(first, count), :].astype(F32)
        act_ref[...] = ((pre + offset_ref[...]) * gate).astype(BF)

    return order(
        kernel,
        [*parts, readin, offset, cutoff],
        [held((count, readin.shape[-1]), BF)],
        scratch=[pltpu.VMEM((count, width), BF)],
        heavy=not near,
    )[0]


def turn(order, acts, parts):
    count, features = acts[0].shape
    rows, width = parts[0][0].shape

    def kernel(w, d, *refs):
        act_refs, part_refs, (turned_ref, tokens_ref) = refs[:2], refs[2:6], refs[6:]
        for half in range(2):
            turned_ref[:, half * count : (half + 1) * count] = act_refs[half][...].T
            for ref, number in zip(part_refs[2 * half : 2 * half + 2], (w[CORE], 1 - w[CORE])):
                tokens_ref[:, span(2 * half + number, rows)] = ref[...].T

    return order(
        kernel,
        [*acts, *parts[0], *parts[1]],
        [held((features, 2 * count), BF), held((width, 2 * count), BF)],
    )


def decode_near(order, away, act, writeout, hidden):
    count, features = act.shape
    blocks = 2
    rows = count // blocks
    dtype = BF if away else F32

    def kernel(w, d, act_ref, weight_ref, hidden_ref, *outs):
        target = 1 - w[CORE] if away else w[CORE]
        live = jnp.where(w[LAYER] <= d[target], 1.0, 0.0)
        out = jnp.dot(act_ref[...], weight_ref[0, target], preferred_element_type=F32)
        less = hidden_ref[target].astype(F32)
        owner = jnp.logical_and(w[LAYER] == 0, w[FEAT] == 0)
        for b, ref in enumerate(outs):
            mine = jnp.where(jnp.logical_and(owner, w[CORE] == b), 1.0, 0.0)
            ref[...] = ((out[b * rows : (b + 1) * rows] - mine * less) * live).astype(dtype)

    outs = [held((rows, writeout.shape[-1]), dtype)] * blocks
    return order(kernel, [act, writeout, hidden], outs)


def decode_far(order, away, other, act, writeout, cuts, heavy=False):
    count, features = act.shape
    rows = count // 2
    part = rows // cuts
    dtype = BF if away else F32

    def kernel(w, d, act_ref, weight_ref, *outs):
        target = 1 - w[CORE] if away else w[CORE]
        live = jnp.where(w[LAYER] <= d[target], 1.0, 0.0)
        block = act_ref[span(1 - w[FEAT] if other else w[FEAT], rows), :]
        out = jnp.dot(block, weight_ref[0, target], preferred_element_type=F32) * live
        for k, ref in enumerate(outs):
            ref[...] = out[k * part : (k + 1) * part].astype(dtype)

    outs = [held((part, writeout.shape[-1]), dtype)] * cuts
    return order(kernel, [act, writeout], outs, heavy=heavy)


def target_gradients(order, mine, scaled, turned, writeout, lo, hi, sens, dec):
    features = writeout.shape[2]
    total, columns = scaled.shape
    block = block_of(features)
    at = lo // columns

    def target(w):
        return w[CORE] if mine else 1 - w[CORE]

    def kernel(w, d, s_ref, turned_ref, weight_ref, *refs):
        dec_ref, out_ref = refs[-2:]
        cols = span(pl.program_id(0), block)
        grad = lax.dot_general(
            s_ref[...],
            weight_ref[0, target(w), cols, lo:hi],
            (((1,), (1,)), ((), ())),
            preferred_element_type=F32,
        )
        out_ref[:, cols] = grad if sens is None else refs[0][:, cols] + grad
        out = jnp.dot(turned_ref[cols, :], s_ref[...], preferred_element_type=F32)
        dec_ref[0, 0] = out.astype(BF)

    operands = [scaled, turned, writeout] + ([] if sens is None else [sens])
    before = [] if dec is None else [dec]
    dec, sens = order(
        kernel,
        operands + before,
        [array(writeout.shape, BF), held((total, features), F32)],
        [HELD] * len(operands) + [ANYWHERE] * len(before),
        [pl.BlockSpec((1, 1, block, columns), lambda i, w, d: (0, target(w), i, at)), HELD],
        grid=(features // block,),
        aliases=[(len(operands), 0)] if before else (),
    )
    order.last = sens
    return dec, sens


def gradients(order, scaled, turned, writeout, lo, hi, sens=None, dec=None, last=None):
    targets, features, width = writeout.shape[1:]
    total, columns = scaled[0].shape
    count = total // 2
    block = block_of(features)
    at = lo // columns

    def kernel(w, d, *refs):
        refs = list(refs)
        s_refs = [refs.pop(0) for _ in range(targets)]
        turned_ref, weight_ref = refs.pop(0), refs.pop(0)
        sens_in = refs.pop(0) if sens is not None else None
        if last is not None:
            cutoff_ref, tokens_ref = refs.pop(0), refs.pop(0)
        if dec is not None:
            refs.pop(0)
        dec_ref = refs.pop(0)
        cols = span(pl.program_id(0), block)
        numbers = [w[CORE], 1 - w[CORE]]
        grad = 0.0 if sens_in is None else sens_in[:, cols]
        for ref, number in zip(s_refs, numbers):
            grad = grad + lax.dot_general(
                ref[...],
                weight_ref[0, number, cols, lo:hi],
                (((1,), (1,)), ((), ())),
                preferred_element_type=F32,
            )
        if last is None:
            refs[0][:, cols] = grad
        else:
            enc_ref, bias_ref, low_ref = refs
            biases = 0.0
            for half, side in enumerate((w[SIDE], 1 - w[SIDE])):
                rows = slice(half * count, (half + 1) * count)
                part = grad[rows] * cutoff_ref[0, span(side, count), cols].astype(F32)
                biases = biases + jnp.sum(part, axis=0, keepdims=True)
                low_ref[rows, :] = part.astype(BF)
            bias_ref[...] = biases
            enc_ref[0] = jnp.dot(
                tokens_ref[...], low_ref[...], preferred_element_type=F32
            ).astype(BF)
        for ref, number in zip(s_refs, numbers):
            out = jnp.dot(turned_ref[cols, :], ref[...], preferred_element_type=F32)
            dec_ref[0, number] = out.astype(BF)

    operands = [*scaled, turned, writeout]
    if sens is not None:
        operands.append(sens)
    if last is not None:
        operands += last
    specs = [HELD] * len(operands)
    aliases = []
    if dec is not None:
        aliases = [(len(operands), 0)]
        operands.append(dec)
        specs.append(ANYWHERE)
    out_specs = [pl.BlockSpec((1, targets, block, columns), lambda i, w, d: (0, 0, i, at))]
    outs = [array(writeout.shape, BF)]
    scratch = []
    if last is not None:
        out_specs.append(pl.BlockSpec((1, width, block), lambda i, w, d: (0, 0, i)))
        out_specs.append(pl.BlockSpec((1, block), lambda i, w, d: (0, i)))
        outs += [array((1, width, features), BF), array((1, features), F32)]
        scratch.append(pltpu.VMEM((total, block), BF))
    else:
        out_specs.append(HELD)
        outs.append(held((total, features), F32))
    results = order(
        kernel, operands, outs, specs, out_specs, (features // block,), scratch, aliases
    )
    if last is None:
        order.last = results[1]
    return results


def pick(flag, a, b):
    return jnp.where(flag, a, b)


def paired_shards(sizes, entries, readin, offset, cutoff, writeout, hidden, depth):
    layers, feats, toks = sizes
    layer, feat, tok = (lax.axis_index(a) for a in ("layer", "feat", "tok"))
    where = jnp.stack([tok // 2, tok % 2, feat, layer]).astype(jnp.int32)
    order = Order((where, depth))

    def to_core(a):
        return lax.ppermute(a, "tok", [(t, t ^ 1) for t in range(toks)])

    def to_side(a):
        return lax.ppermute(a, "tok", [(t, t ^ 2) for t in range(toks)])

    def mixed(first):
        pairs = []
        for f in range(feats):
            for t in range(toks):
                over_side = (t % 2 == 0) == first
                goal = (f, t ^ 2) if over_side else (f ^ 1, t)
                pairs.append((f * toks + t, goal[0] * toks + goal[1]))
        return lambda a: lax.ppermute(a, ("feat", "tok"), pairs)

    to_first, to_second = mixed(True), mixed(False)
    binary = layers & (layers - 1) == 0

    def layer_goal(l, s):
        return l ^ s if binary else lax.rem(l + s, layers)

    def layer_source(l, s):
        return l ^ s if binary else lax.rem(l - s + layers, layers)

    def to_layer(a, s):
        return lax.ppermute(
            a, "layer", [(l, l ^ s if binary else (l + s) % layers) for l in range(layers)]
        )

    own = entries[0]
    rows, width = own.shape
    total = rows * toks
    inverse = 1.0 / math.sqrt(total)
    piece = rows // layers
    chunks = column_chunks(width)

    far = to_side(own)
    near = to_core(own)
    readin, cutoff, writeout, hidden = load(order, readin, cutoff, writeout, hidden)
    act_near = encode(order, True, (own, near), readin, offset, cutoff)

    away = decode_near(order, True, act_near, writeout, hidden)
    here_got = [to_core(a) for a in away]
    here = [*decode_near(order, False, act_near, writeout, hidden), *here_got]
    far = order.pass_on(far)

    def first_kernel(w, d, kept0, kept1, got0, got1, *outs):
        y1 = w[FEAT] == 1
        other = pick(y1, kept0[...], kept1[...]) + pick(y1, got0[...], got1[...]).astype(F32)
        for (lo, hi), out in zip(chunks, outs):
            out[...] = other[:, lo:hi].astype(BF)

    sends = order(first_kernel, here, [held((rows, hi - lo), BF) for lo, hi in chunks])
    got_first = [to_first(send) for send in sends]

    far_near = to_core(far)
    act_far = encode(order, False, (far, far_near), readin, offset, cutoff)

    def far_block(other, cuts):
        away = decode_far(order, True, other, act_far, writeout, cuts)
        got = [to_core(a) for a in away]
        return (*decode_far(order, False, other, act_far, writeout, 1), *got)

    def joined_rows(refs, at):
        return jnp.concatenate([ref[:, at] for ref in refs]).astype(F32)

    there_other = far_block(True, 2)

    def reduce_sides(lo, hi, got_first, heavy):
        size = hi - lo
        at = slice(lo, hi)

        def second_kernel(w, d, hk0, hk1, hg0, hg1, first, tk, *refs):
            *tg, out_first, out_second = refs
            y0 = w[FEAT] == 0
            here_y = pick(y0, hk0[:, at], hk1[:, at])
            here_y += pick(y0, hg0[:, at], hg1[:, at]).astype(F32)
            there_other = tk[:, at] + joined_rows(tg, at)
            zero = w[CORE] == 0
            out_first[...] = pick(zero, here_y, there_other).astype(BF)
            rest = pick(zero, there_other, here_y) + first[...].astype(F32)
            out_second[...] = rest.astype(BF)

        operands = (*here, got_first, *there_other)
        sends = order(second_kernel, operands, [held((rows, size), BF)] * 2, heavy=heavy)
        return lo, hi, to_first(sends[0]), to_second(sends[1])

    def send_pieces(lo, hi, got, got_second, heavy):
        size = hi - lo

        def kernel(w, d, *refs):
            tk, *tg = refs[: len(there)]
            first, second, mine, *outs, kept = refs[len(there) :]
            kept[...] = (
                tk[:, lo:hi]
                + joined_rows(tg, slice(lo, hi))
                + first[...].astype(F32)
                + second[...].astype(F32)
            )
            mine[...] = kept[span(w[LAYER], piece), :]
            for s, out in enumerate(outs, 1):
                out[...] = kept[span(layer_goal(w[LAYER], s), piece), :].astype(BF)

        outs = [held((piece, size), F32)] + [held((piece, size), BF)] * (layers - 1)
        scratch = [pltpu.VMEM((rows, size), F32)]
        mine, *outs = order(
            kernel, (*there, got, got_second), outs, scratch=scratch, heavy=heavy
        )
        return mine, [to_layer(out, s) for s, out in enumerate(outs, 1)]

    def scale_piece(mine, pieces):
        def kernel(w, d, mine_ref, *refs):
            *refs, out = refs
            value = mine_ref[...]
            for ref in refs:
                value = value + ref[...].astype(F32)
            out[...] = (value * inverse).astype(BF)

        scaled = order(kernel, (mine, *pieces), [held(mine.shape, BF)], heavy=True)[0]
        return scaled, [to_layer(scaled, s) for s in range(1, layers)]

    def join_pieces(scaled, pieces, wait):
        size = scaled.shape[1]

        def kernel(w, d, *refs):
            *refs, out = refs
            out[span(w[LAYER], piece), :] = refs[0][...]
            for s, ref in enumerate(refs[1:], 1):
                out[span(layer_source(w[LAYER], s), piece), :] = ref[...]

        outs = [held((rows, size), BF)]
        done = order(kernel, (scaled, *pieces), outs, heavy=True, wait=wait)[0]
        got_second, got_first = to_second(done), to_first(done)
        return done, got_second, got_first, to_first(got_second)

    def join_all(*blocks):
        size = blocks[0].shape[1]

        def kernel(w, d, *refs):
            *refs, out = refs
            y = w[FEAT]
            zero = w[CORE] == 0
            live = jnp.where(w[LAYER] <= d[w[CORE]], 1.0, 0.0).astype(BF)
            numbers = (2 + y, pick(zero, 3 - y, y), pick(zero, y, 3 - y), 1 - y)
            for ref, number in zip(refs, numbers):
                out[span(number, rows), :] = ref[...] * live

        full = order(kernel, blocks, [held((total, size), BF)], heavy=True)[0]
        return full, to_core(full)

    reduced = [
        reduce_sides(*chunk, got, k > 0) for k, (chunk, got) in enumerate(zip(chunks, got_first))
    ]
    there = far_block(False, 4)
    turned, tokens = turn(order, (act_near, act_far), ((own, near), (far, far_near)))
    order.keep = [writeout, cutoff, turned, tokens]
    count = len(chunks)
    sent, joined = send_pieces(*reduced[0], False), []
    for k in range(count):
        scaled = scale_piece(*sent)
        if k + 1 < count:
            sent = send_pieces(*reduced[k + 1], True)
        joined.append(join_pieces(*scaled, [joined[k - 1][2]] if k > 0 else []))
    scaled = join_all(*joined[0])
    sens = dec = None
    for k, (lo, hi) in enumerate(chunks[:-1]):
        own, other = scaled
        dec, sens = target_gradients(order, True, own, turned, writeout, lo, hi, sens, dec)
        following = join_all(*joined[k + 1])
        dec, sens = target_gradients(order, False, other, turned, writeout, lo, hi, sens, dec)
        scaled = following
    order.keep = []
    lo, hi = chunks[-1]
    dec, enc, bias = gradients(
        order, scaled, turned, writeout, lo, hi, sens, dec, (cutoff, tokens)
    )
    return enc, dec, bias


def solution(mesh):
    sizes = tuple(mesh.shape[a] for a in ("layer", "feat", "tok"))

    def shards(*args):
        rows = args[0].shape[1]
        targets = args[4].shape[1]
        paired = sizes[1] == targets == 2 and sizes[2] == 4
        if paired and rows % ROWS_UNIT == 0 and rows % (16 * sizes[0]) == 0:
            return paired_shards(sizes, *args)
        return plain_shards(*args)

    return jax.shard_map(
        shards,
        mesh=mesh,
        in_specs=(
            P("layer", "tok", None),
            P("layer", None, ("feat", "tok")),
            P("layer", ("feat", "tok")),
            P("layer", None, ("feat", "tok")),
            P("layer", None, ("feat", "tok"), None),
            P(None, "tok", None),
            P(),
        ),
        out_specs=(
            P("layer", None, ("feat", "tok")),
            P("layer", None, ("feat", "tok"), None),
            P("layer", ("feat", "tok")),
        ),
        check_vma=False,
    )
```

```python
import math

import jax
import jax.numpy as jnp
from jax import lax
from jax.experimental import pallas as pl
from jax.experimental.pallas import tpu as pltpu
from jax.sharding import PartitionSpec as P

BF = jnp.bfloat16
F32 = jnp.float32


def plain_shards(entries, readin, offset, cutoff, writeout, hidden, depth):
    layer = lax.axis_index("layer")
    owner = jnp.logical_and(layer == 0, lax.axis_index("feat") == 0).astype(F32)
    gathered = lax.all_gather(entries, "tok", axis=1, tiled=True)[0]
    inverse = 1.0 / math.sqrt(gathered.shape[0])
    gate = cutoff[0].astype(F32)
    pre = jnp.dot(gathered, readin[0], preferred_element_type=F32) + offset[0][None, :]
    act = (pre * gate).astype(BF)
    live = (layer <= depth).astype(F32)
    targets = writeout.shape[1]
    partials = jnp.stack(
        [jnp.dot(act, writeout[0, t], preferred_element_type=F32) for t in range(targets)]
    )
    rows = hidden.shape[1]
    start = lax.axis_index("tok") * rows
    current = lax.dynamic_slice_in_dim(partials, start, rows, 1)
    partials = lax.dynamic_update_slice_in_dim(
        partials, current - owner * hidden.astype(F32), start, 1
    )
    summed = lax.psum_scatter(
        partials * live[:, None, None], ("feat", "tok"), scatter_dimension=1, tiled=True
    )
    summed = lax.psum(summed, "layer")
    scaled = lax.all_gather((summed * inverse).astype(BF), ("feat", "tok"), axis=1, tiled=True)
    dec = [
        (jnp.einsum("tf,td->fd", act, scaled[t], preferred_element_type=F32) * live[t]).astype(BF)
        for t in range(targets)
    ]
    sens = sum(
        live[t] * jnp.einsum("td,fd->tf", scaled[t], writeout[0, t], preferred_element_type=F32)
        for t in range(targets)
    )
    pre_grad = sens * gate
    enc = jnp.einsum("td,tf->df", gathered, pre_grad.astype(BF), preferred_element_type=F32)
    return enc.astype(BF)[None], jnp.stack(dec)[None], jnp.sum(pre_grad, axis=0)[None]


def column_chunks(width):
    for parts in (3, 2):
        if width % (128 * parts) == 0:
            unit = width // parts
            return [(0, width - unit), (width - unit, width)]
    return [(0, width)]


VMEM_MIB = 16
FEATURE_BLOCK = 512
ROWS_UNIT = 128
HEAVY = 10**11
SIDE, CORE, FEAT, LAYER = range(4)
HELD = pl.BlockSpec(memory_space=pltpu.VMEM)
ANYWHERE = pl.BlockSpec(memory_space=pl.ANY)


def held(shape, dtype):
    return pltpu.VMEM(shape, dtype)


def array(shape, dtype):
    return jax.ShapeDtypeStruct(shape, dtype)


def block_of(features):
    return FEATURE_BLOCK if features % FEATURE_BLOCK == 0 else features


def span(number, size):
    return pl.ds(pl.multiple_of(number * size, size), size)


class Order:
    def __init__(self, scalars):
        self.scalars = scalars
        self.last = None
        self.keep = []

    def __call__(
        self,
        kernel,
        operands,
        outs,
        specs=None,
        out_specs=None,
        grid=(1,),
        scratch=(),
        aliases=(),
        heavy=False,
        wait=(),
    ):
        count = len(operands)
        operands = list(operands)
        specs = list(specs or [HELD] * count)
        waits = [*([] if self.last is None else [self.last]), *wait]
        keep = [k for k in self.keep if all(k is not o for o in operands)]

        def body(*refs):
            at = len(self.scalars) + count
            kernel(*refs[:at], *refs[at + len(waits) + len(keep) :])

        results = pl.pallas_call(
            body,
            grid_spec=pltpu.PrefetchScalarGridSpec(
                num_scalar_prefetch=len(self.scalars),
                grid=grid,
                in_specs=specs + [ANYWHERE] * len(waits) + [HELD] * len(keep),
                out_specs=list(out_specs or [HELD] * len(outs)),
                scratch_shapes=list(scratch),
            ),
            out_shape=list(outs),
            input_output_aliases={len(self.scalars) + i: o for i, o in aliases},
            compiler_params=pltpu.CompilerParams(vmem_limit_bytes=VMEM_MIB * 1024 * 1024),
            cost_estimate=pl.CostEstimate(
                flops=HEAVY if heavy else 1000, bytes_accessed=1000, transcendentals=0
            ),
        )(*self.scalars, *operands, *waits, *keep)
        self.last = results[0]
        return results


def load(order, *operands):
    parts = []
    for k, o in enumerate(operands):
        axis = max(range(o.ndim - 1), key=lambda i: o.shape[i])
        cuts = 4 if o.shape[axis] % 64 == 0 else 1
        size = o.shape[axis] // cuts
        for c in range(cuts):
            parts.append((k, (slice(None),) * axis + (pl.ds(c * size, size),)))

    def kernel(w, d, *refs):
        *refs, sems = refs
        n = len(operands)
        copies = [
            pltpu.make_async_copy(refs[k].at[at], refs[n + k].at[at], sems.at[i])
            for i, (k, at) in enumerate(parts)
        ]
        for copy in copies:
            copy.start()
        for copy in copies:
            copy.wait()

    return order(
        kernel,
        [pltpu.with_memory_space_constraint(o, pltpu.HBM) for o in operands],
        [held(o.shape, o.dtype) for o in operands],
        specs=[pl.BlockSpec(memory_space=pltpu.HBM)] * len(operands),
        scratch=[pltpu.SemaphoreType.DMA((len(parts),))],
        heavy=True,
    )


def encode(order, near, parts, readin, offset, cutoff):
    rows, width = parts[0].shape
    count = 2 * rows

    def kernel(w, d, own_ref, other_ref, readin_ref, offset_ref, cutoff_ref, act_ref, both):
        for ref, number in ((own_ref, w[CORE]), (other_ref, 1 - w[CORE])):
            both[span(number, rows), :] = ref[...]
        first = w[SIDE] if near else 1 - w[SIDE]
        pre = jnp.dot(both[...], readin_ref[0], preferred_element_type=F32)
        gate = cutoff_ref[0, span(first, count), :].astype(F32)
        act_ref[...] = ((pre + offset_ref[...]) * gate).astype(BF)

    return order(
        kernel,
        [*parts, readin, offset, cutoff],
        [held((count, readin.shape[-1]), BF)],
        scratch=[pltpu.VMEM((count, width), BF)],
        heavy=not near,
    )[0]


def turn(order, acts, parts):
    count, features = acts[0].shape
    rows, width = parts[0][0].shape

    def kernel(w, d, *refs):
        act_refs, part_refs, (turned_ref, tokens_ref) = refs[:2], refs[2:6], refs[6:]
        for half in range(2):
            turned_ref[:, half * count : (half + 1) * count] = act_refs[half][...].T
            for ref, number in zip(part_refs[2 * half : 2 * half + 2], (w[CORE], 1 - w[CORE])):
                tokens_ref[:, span(2 * half + number, rows)] = ref[...].T

    return order(
        kernel,
        [*acts, *parts[0], *parts[1]],
        [held((features, 2 * count), BF), held((width, 2 * count), BF)],
    )


def decode_near(order, away, act, writeout, hidden):
    count, features = act.shape
    blocks = 2
    rows = count // blocks
    dtype = BF if away else F32

    def kernel(w, d, act_ref, weight_ref, hidden_ref, *outs):
        target = 1 - w[CORE] if away else w[CORE]
        live = jnp.where(w[LAYER] <= d[target], 1.0, 0.0)
        out = jnp.dot(act_ref[...], weight_ref[0, target], preferred_element_type=F32)
        less = hidden_ref[target].astype(F32)
        owner = jnp.logical_and(w[LAYER] == 0, w[FEAT] == 0)
        for b, ref in enumerate(outs):
            mine = jnp.where(jnp.logical_and(owner, w[CORE] == b), 1.0, 0.0)
            ref[...] = ((out[b * rows : (b + 1) * rows] - mine * less) * live).astype(dtype)

    outs = [held((rows, writeout.shape[-1]), dtype)] * blocks
    return order(kernel, [act, writeout, hidden], outs)


def decode_far(order, away, other, act, writeout, cuts, heavy=False):
    count, features = act.shape
    rows = count // 2
    part = rows // cuts
    dtype = BF if away else F32

    def kernel(w, d, act_ref, weight_ref, *outs):
        target = 1 - w[CORE] if away else w[CORE]
        live = jnp.where(w[LAYER] <= d[target], 1.0, 0.0)
        block = act_ref[span(1 - w[FEAT] if other else w[FEAT], rows), :]
        out = jnp.dot(block, weight_ref[0, target], preferred_element_type=F32) * live
        for k, ref in enumerate(outs):
            ref[...] = out[k * part : (k + 1) * part].astype(dtype)

    outs = [held((part, writeout.shape[-1]), dtype)] * cuts
    return order(kernel, [act, writeout], outs, heavy=heavy)


def target_gradients(order, mine, scaled, turned, writeout, lo, hi, sens, dec):
    features = writeout.shape[2]
    total, columns = scaled.shape
    block = block_of(features)
    at = lo // columns

    def target(w):
        return w[CORE] if mine else 1 - w[CORE]

    def kernel(w, d, s_ref, turned_ref, weight_ref, *refs):
        dec_ref, out_ref = refs[-2:]
        cols = span(pl.program_id(0), block)
        grad = lax.dot_general(
            s_ref[...],
            weight_ref[0, target(w), cols, lo:hi],
            (((1,), (1,)), ((), ())),
            preferred_element_type=F32,
        )
        out_ref[:, cols] = grad if sens is None else refs[0][:, cols] + grad
        out = jnp.dot(turned_ref[cols, :], s_ref[...], preferred_element_type=F32)
        dec_ref[0, 0] = out.astype(BF)

    operands = [scaled, turned, writeout] + ([] if sens is None else [sens])
    before = [] if dec is None else [dec]
    dec, sens = order(
        kernel,
        operands + before,
        [array(writeout.shape, BF), held((total, features), F32)],
        [HELD] * len(operands) + [ANYWHERE] * len(before),
        [pl.BlockSpec((1, 1, block, columns), lambda i, w, d: (0, target(w), i, at)), HELD],
        grid=(features // block,),
        aliases=[(len(operands), 0)] if before else (),
    )
    order.last = sens
    return dec, sens


def gradients(order, scaled, turned, writeout, lo, hi, sens=None, dec=None, last=None):
    targets, features, width = writeout.shape[1:]
    total, columns = scaled[0].shape
    count = total // 2
    block = block_of(features)
    at = lo // columns

    def kernel(w, d, *refs):
        refs = list(refs)
        s_refs = [refs.pop(0) for _ in range(targets)]
        turned_ref, weight_ref = refs.pop(0), refs.pop(0)
        sens_in = refs.pop(0) if sens is not None else None
        if last is not None:
            cutoff_ref, tokens_ref = refs.pop(0), refs.pop(0)
        if dec is not None:
            refs.pop(0)
        dec_ref = refs.pop(0)
        cols = span(pl.program_id(0), block)
        numbers = [w[CORE], 1 - w[CORE]]
        grad = 0.0 if sens_in is None else sens_in[:, cols]
        for ref, number in zip(s_refs, numbers):
            grad = grad + lax.dot_general(
                ref[...],
                weight_ref[0, number, cols, lo:hi],
                (((1,), (1,)), ((), ())),
                preferred_element_type=F32,
            )
        if last is None:
            refs[0][:, cols] = grad
        else:
            enc_ref, bias_ref, low_ref = refs
            biases = 0.0
            for half, side in enumerate((w[SIDE], 1 - w[SIDE])):
                rows = slice(half * count, (half + 1) * count)
                part = grad[rows] * cutoff_ref[0, span(side, count), cols].astype(F32)
                biases = biases + jnp.sum(part, axis=0, keepdims=True)
                low_ref[rows, :] = part.astype(BF)
            bias_ref[...] = biases
            enc_ref[0] = jnp.dot(
                tokens_ref[...], low_ref[...], preferred_element_type=F32
            ).astype(BF)
        for ref, number in zip(s_refs, numbers):
            out = jnp.dot(turned_ref[cols, :], ref[...], preferred_element_type=F32)
            dec_ref[0, number] = out.astype(BF)

    operands = [*scaled, turned, writeout]
    if sens is not None:
        operands.append(sens)
    if last is not None:
        operands += last
    specs = [HELD] * len(operands)
    aliases = []
    if dec is not None:
        aliases = [(len(operands), 0)]
        operands.append(dec)
        specs.append(ANYWHERE)
    out_specs = [pl.BlockSpec((1, targets, block, columns), lambda i, w, d: (0, 0, i, at))]
    outs = [array(writeout.shape, BF)]
    scratch = []
    if last is not None:
        out_specs.append(pl.BlockSpec((1, width, block), lambda i, w, d: (0, 0, i)))
        out_specs.append(pl.BlockSpec((1, block), lambda i, w, d: (0, i)))
        outs += [array((1, width, features), BF), array((1, features), F32)]
        scratch.append(pltpu.VMEM((total, block), BF))
    else:
        out_specs.append(HELD)
        outs.append(held((total, features), F32))
    results = order(
        kernel, operands, outs, specs, out_specs, (features // block,), scratch, aliases
    )
    if last is None:
        order.last = results[1]
    return results


def pick(flag, a, b):
    return jnp.where(flag, a, b)


def paired_shards(sizes, entries, readin, offset, cutoff, writeout, hidden, depth):
    layers, feats, toks = sizes
    layer, feat, tok = (lax.axis_index(a) for a in ("layer", "feat", "tok"))
    where = jnp.stack([tok // 2, tok % 2, feat, layer]).astype(jnp.int32)
    order = Order((where, depth))

    def to_core(a):
        return lax.ppermute(a, "tok", [(t, t ^ 1) for t in range(toks)])

    def to_side(a):
        return lax.ppermute(a, "tok", [(t, t ^ 2) for t in range(toks)])

    def mixed(first):
        pairs = []
        for f in range(feats):
            for t in range(toks):
                over_side = (t % 2 == 0) == first
                goal = (f, t ^ 2) if over_side else (f ^ 1, t)
                pairs.append((f * toks + t, goal[0] * toks + goal[1]))
        return lambda a: lax.ppermute(a, ("feat", "tok"), pairs)

    to_first, to_second = mixed(True), mixed(False)
    binary = layers & (layers - 1) == 0

    def layer_goal(l, s):
        return l ^ s if binary else lax.rem(l + s, layers)

    def layer_source(l, s):
        return l ^ s if binary else lax.rem(l - s + layers, layers)

    def to_layer(a, s):
        return lax.ppermute(
            a, "layer", [(l, l ^ s if binary else (l + s) % layers) for l in range(layers)]
        )

    own = entries[0]
    rows, width = own.shape
    total = rows * toks
    inverse = 1.0 / math.sqrt(total)
    piece = rows // layers
    chunks = column_chunks(width)

    far = to_side(own)
    near = to_core(own)
    readin, cutoff, writeout, hidden = load(order, readin, cutoff, writeout, hidden)
    act_near = encode(order, True, (own, near), readin, offset, cutoff)

    away = decode_near(order, True, act_near, writeout, hidden)
    here_got = [to_core(a) for a in away]
    here = [*decode_near(order, False, act_near, writeout, hidden), *here_got]

    def first_kernel(w, d, kept0, kept1, got0, got1, far_ref, *outs):
        y1 = w[FEAT] == 1
        other = pick(y1, kept0[...], kept1[...]) + pick(y1, got0[...], got1[...]).astype(F32)
        for (lo, hi), out in zip(chunks, outs):
            out[...] = other[:, lo:hi].astype(BF)

    *sends, far = order(
        first_kernel,
        [*here, far],
        [held((rows, hi - lo), BF) for lo, hi in chunks] + [array(far.shape, BF)],
        [HELD] * len(here) + [ANYWHERE],
        [HELD] * len(chunks) + [ANYWHERE],
        aliases=[(len(here), len(chunks))],
    )
    got_first = [to_first(send) for send in sends]

    far_near = to_core(far)
    act_far = encode(order, False, (far, far_near), readin, offset, cutoff)

    def far_block(other, cuts):
        away = decode_far(order, True, other, act_far, writeout, cuts)
        got = [to_core(a) for a in away]
        return (*decode_far(order, False, other, act_far, writeout, 1), *got)

    def joined_rows(refs, at):
        return jnp.concatenate([ref[:, at] for ref in refs]).astype(F32)

    there_other = far_block(True, 2)

    def reduce_sides(lo, hi, got_first, heavy):
        size = hi - lo
        at = slice(lo, hi)

        def second_kernel(w, d, hk0, hk1, hg0, hg1, first, tk, *refs):
            *tg, out_first, out_second = refs
            y0 = w[FEAT] == 0
            here_y = pick(y0, hk0[:, at], hk1[:, at])
            here_y += pick(y0, hg0[:, at], hg1[:, at]).astype(F32)
            there_other = tk[:, at] + joined_rows(tg, at)
            zero = w[CORE] == 0
            out_first[...] = pick(zero, here_y, there_other).astype(BF)
            rest = pick(zero, there_other, here_y) + first[...].astype(F32)
            out_second[...] = rest.astype(BF)

        operands = (*here, got_first, *there_other)
        sends = order(second_kernel, operands, [held((rows, size), BF)] * 2, heavy=heavy)
        return lo, hi, to_first(sends[0]), to_second(sends[1])

    def send_pieces(lo, hi, got, got_second, heavy):
        size = hi - lo

        def kernel(w, d, *refs):
            tk, *tg = refs[: len(there)]
            first, second, mine, *outs, kept = refs[len(there) :]
            kept[...] = (
                tk[:, lo:hi]
                + joined_rows(tg, slice(lo, hi))
                + first[...].astype(F32)
                + second[...].astype(F32)
            )
            mine[...] = kept[span(w[LAYER], piece), :]
            for s, out in enumerate(outs, 1):
                out[...] = kept[span(layer_goal(w[LAYER], s), piece), :].astype(BF)

        outs = [held((piece, size), F32)] + [held((piece, size), BF)] * (layers - 1)
        scratch = [pltpu.VMEM((rows, size), F32)]
        mine, *outs = order(
            kernel, (*there, got, got_second), outs, scratch=scratch, heavy=heavy
        )
        return mine, [to_layer(out, s) for s, out in enumerate(outs, 1)]

    def scale_piece(mine, pieces):
        def kernel(w, d, mine_ref, *refs):
            *refs, out = refs
            value = mine_ref[...]
            for ref in refs:
                value = value + ref[...].astype(F32)
            out[...] = (value * inverse).astype(BF)

        scaled = order(kernel, (mine, *pieces[::-1]), [held(mine.shape, BF)], heavy=True)[0]
        return scaled, [to_layer(scaled, s) for s in range(1, layers)]

    def join_pieces(scaled, pieces, wait):
        size = scaled.shape[1]

        def kernel(w, d, *refs):
            *refs, out = refs
            out[span(w[LAYER], piece), :] = refs[0][...]
            for s, ref in enumerate(refs[:0:-1], 1):
                out[span(layer_source(w[LAYER], s), piece), :] = ref[...]

        outs = [held((rows, size), BF)]
        done = order(kernel, (scaled, *pieces[::-1]), outs, heavy=True, wait=wait)[0]
        got_second, got_first = to_second(done), to_first(done)
        return done, got_second, got_first, to_first(got_second)

    def join_all(*blocks):
        size = blocks[0].shape[1]

        def kernel(w, d, *refs):
            *refs, out = refs
            y = w[FEAT]
            zero = w[CORE] == 0
            live = jnp.where(w[LAYER] <= d[w[CORE]], 1.0, 0.0).astype(BF)
            numbers = (2 + y, pick(zero, 3 - y, y), pick(zero, y, 3 - y), 1 - y)
            for ref, number in zip(refs, numbers):
                out[span(number, rows), :] = ref[...] * live

        full = order(kernel, blocks, [held((total, size), BF)], heavy=True)[0]
        return full, to_core(full)

    reduced = [
        reduce_sides(*chunk, got, k > 0) for k, (chunk, got) in enumerate(zip(chunks, got_first))
    ]
    there = far_block(False, 4)
    turned, tokens = turn(order, (act_near, act_far), ((own, near), (far, far_near)))
    order.keep = [writeout, cutoff, turned, tokens]
    count = len(chunks)
    sent, joined = send_pieces(*reduced[0], False), []
    for k in range(count):
        scaled = scale_piece(*sent)
        if k + 1 < count:
            sent = send_pieces(*reduced[k + 1], True)
        joined.append(join_pieces(*scaled, [joined[k - 1][2]] if k > 0 else []))
    scaled = join_all(*joined[0])
    sens = dec = None
    for k, (lo, hi) in enumerate(chunks[:-1]):
        own, other = scaled
        dec, sens = target_gradients(order, True, own, turned, writeout, lo, hi, sens, dec)
        following = join_all(*joined[k + 1])
        dec, sens = target_gradients(order, False, other, turned, writeout, lo, hi, sens, dec)
        scaled = following
    order.keep = []
    lo, hi = chunks[-1]
    dec, enc, bias = gradients(
        order, scaled, turned, writeout, lo, hi, sens, dec, (cutoff, tokens)
    )
    return enc, dec, bias


def solution(mesh):
    sizes = tuple(mesh.shape[a] for a in ("layer", "feat", "tok"))

    def shards(*args):
        rows = args[0].shape[1]
        targets = args[4].shape[1]
        paired = sizes[1] == targets == 2 and sizes[2] == 4
        if paired and rows % ROWS_UNIT == 0 and rows % (16 * sizes[0]) == 0:
            return paired_shards(sizes, *args)
        return plain_shards(*args)

    return jax.shard_map(
        shards,
        mesh=mesh,
        in_specs=(
            P("layer", "tok", None),
            P("layer", None, ("feat", "tok")),
            P("layer", ("feat", "tok")),
            P("layer", None, ("feat", "tok")),
            P("layer", None, ("feat", "tok"), None),
            P(None, "tok", None),
            P(),
        ),
        out_specs=(
            P("layer", None, ("feat", "tok")),
            P("layer", None, ("feat", "tok"), None),
            P("layer", ("feat", "tok")),
        ),
        check_vma=False,
    )
```
